128 devices in a mesh: comp: 8 (over x, core), blk: 16 (over y, z).
Axes of the slice: x: 4, y: 4, z: 4, core: 2. Of those that a mesh axis runs over, the one named last changes fastest.
Arguments:
- start_modes: float32 [8, 65536, 256], P('comp', 'blk')
- stiff_diag: float32 [8, 512, 128, 128], P('comp', 'blk')
- stiff_off: float32 [8, 512, 128, 128], P('comp', 'blk'), may hold values from -0.625 to 0.625
- mass_blocks: float32 [8, 512, 128, 128], P('comp', 'blk')
- coupling: float32 [8, 512, 128, 128], P('comp', 'blk'), may hold values from -6 to 6
- interface_block: int32 [8, 512], P('comp', 'blk'), may hold values from 0 to 16
- global_iface: int32 [8, 16], P('comp'), may hold values from 0 to 31
Outputs:
- modes: float32 [8, 65536, 256], P('comp', 'blk')
- reduced_stiffness: float32 [8, 256, 256], P('comp')
- assembled: float32 [32, 128, 128], P('comp')
The draws below stay inside these ranges and needn't reach their ends.
All inputs are finite; a program needn't handle non-finite values.
Results may differ from the reference program's by a relative error of at most 0.0003.
Values sent between devices are 32-bit elements; how exact they have to be, the bound alone decides.
A program may use at most 128 MiB of HBM per device.

```python
import math
import jax
import jax.numpy as jnp
import numpy as np
from jax import lax

BS = 128
MODES = 256
ITERS = 2
COMPS = 8
NBLK = 512
NIF = 16
GIF = 32


def region_soft(key):
    return jax.random.randint(jax.random.fold_in(key, 5), (COMPS, NBLK), 0, 2)


def draw_start_modes(key, part):
    soft_rows = region_soft(key).reshape(COMPS, NBLK, 1, 1)
    character = jax.random.randint(jax.random.fold_in(key, 31), (COMPS, 1, 1, MODES + 1), 0, 2)
    weight = jnp.where(soft_rows == character, 1.0, 0.25).astype(jnp.float32)
    noise = jax.random.normal(jax.random.fold_in(key, 32), (COMPS, NBLK, BS, MODES + 1), jnp.float32)
    columns = noise * weight
    mixing = jax.random.uniform(jax.random.fold_in(key, 33), (COMPS, 1, 1, MODES), jnp.float32, -0.8, 0.8)
    mixed = columns[:, :, :, :MODES] + mixing * columns[:, :, :, 1:]
    return jnp.clip(mixed, -6.0, 6.0).reshape(COMPS, NBLK * BS, MODES)


def draw_stiff_diag(key, part):
    random_part = jax.random.normal(jax.random.fold_in(key, 11), (COMPS, NBLK, BS, BS), jnp.float32)
    symmetric = (random_part + jnp.swapaxes(random_part, 2, 3)) * (0.6 / (2.0 * BS) ** 0.5)
    soft_rows = region_soft(key).reshape(COMPS, NBLK, 1, 1)
    soft_level = jnp.full((COMPS, NBLK, 1, 1), 2.8, jnp.float32)
    stiff_level = jnp.full((COMPS, NBLK, 1, 1), 11.0, jnp.float32)
    diag_level = jnp.where(soft_rows == 1, soft_level, stiff_level)
    return symmetric + diag_level * jnp.eye(BS, dtype=jnp.float32)


def draw_mass_blocks(key, part):
    random_part = jax.random.normal(jax.random.fold_in(key, 21), (COMPS, NBLK, BS, BS), jnp.float32)
    symmetric = (random_part + jnp.swapaxes(random_part, 2, 3)) * (0.3 / (2.0 * BS) ** 0.5)
    diag_level = jnp.ones((COMPS, NBLK, 1, 1), jnp.float32)
    return symmetric + diag_level * jnp.eye(BS, dtype=jnp.float32)


def place_ends(values, rng, smallest, largest):
    longest = values.shape.index(max(values.shape))
    spots = []
    for shift in (0, 1):
        where = [jax.random.randint(jax.random.fold_in(rng, axis), (), 0, length) for axis, length in enumerate(values.shape)]
        where[longest] = (where[longest] + shift) % values.shape[longest]
        spots.append(tuple(where))
    return values.at[spots[0]].set(smallest).at[spots[1]].set(largest)


def levels(stream_key, extent, shards, smallest, top_value):
    def one(axis_at, blocks):
        heights = jax.random.uniform(jax.random.fold_in(jax.random.fold_in(stream_key, 6), axis_at), (blocks,), jnp.float32, smallest / len(shards), top_value / len(shards))
        return jnp.repeat(jnp.exp(heights), extent[axis_at] // blocks).reshape((-1,) + (1,) * (len(extent) - axis_at - 1))

    level = one(*shards[0])
    for cut in shards[1:]:
        level = level * one(*cut)
    return level


def rank_table(amount, lean):
    loads = [(1 << 20) // math.isqrt(standing ** lean) + 1 for standing in range(1, amount + 1)]
    width = 1 + sum(loads) // (1 << 30)
    return np.cumsum(np.array([max(1, weight // width) for weight in loads]))


def ranked_ids(key, extent, number_of, slope):
    listing = rank_table(number_of, slope)
    pick = jax.random.randint(jax.random.fold_in(key, 1), extent, 0, int(listing[number_of - 1]))
    standing = jnp.searchsorted(jnp.asarray(listing, jnp.int32), pick, side="right")
    return jax.random.permutation(jax.random.fold_in(key, 2), number_of)[standing].astype(jnp.int32)


def scatter_about(rng, extent, spread, most, cuts=(), kind=jnp.bfloat16):
    factor_of = levels(rng, extent, cuts, -0.22, 0.18) if cuts else 1.0
    drawn = jax.random.normal(rng, extent, jnp.float32) * spread * factor_of
    return jnp.minimum(jnp.maximum(drawn, -most), most).astype(kind)


def setup_inputs(seed: int = 0) -> dict:
    key_list = jax.random.split(jax.random.key(seed), 8)
    start_modes = draw_start_modes(jax.random.fold_in(key_list[7], 71), 0)
    stiff_diag = draw_stiff_diag(jax.random.fold_in(key_list[7], 71), 0)
    stiff_off = scatter_about(key_list[2], (COMPS, NBLK, BS, BS), (0.45 / BS ** 0.5), 0.625, ((0, 8), (1, 16)), jnp.float32)
    mass_blocks = draw_mass_blocks(jax.random.fold_in(key_list[7], 71), 0)
    coupling = scatter_about(key_list[4], (COMPS, NBLK, BS, BS), 1.0, 6.0, ((0, 8), (1, 16)), jnp.float32)
    interface_block = place_ends(jax.random.randint(key_list[5], (COMPS, NBLK), 0, NIF + 1), jax.random.fold_in(key_list[5], 1), 0, NIF).astype(jnp.int32)
    global_iface = place_ends(ranked_ids(key_list[6], (COMPS, NIF), GIF, 2), jax.random.fold_in(key_list[6], 3), 0, GIF - 1).astype(jnp.int32)
    return dict(start_modes=start_modes, stiff_diag=stiff_diag, stiff_off=stiff_off, mass_blocks=mass_blocks, coupling=coupling, interface_block=interface_block, global_iface=global_iface)


highest = lax.Precision.HIGHEST
step_size = 0.15

def block_product(blocks, vectors):
    return jnp.einsum('bij,bjm->bim', blocks, vectors, precision=highest)

def stiff_apply(stiff_self, stiff_link, vectors):
    zero_block = jnp.zeros_like(vectors[:1])
    preceding = jnp.concatenate([zero_block, vectors[:-1]], 0)
    following = jnp.concatenate([vectors[1:], zero_block], 0)
    link_after = jnp.concatenate([stiff_link[1:], jnp.zeros_like(stiff_link[:1])], 0)
    result = block_product(stiff_self, vectors) + block_product(stiff_link, preceding)
    return result + jnp.einsum('bji,bjm->bim', link_after, following, precision=highest)

def lower_inverse(matrix):
    factor = jnp.linalg.cholesky(matrix)
    unit_matrix = jnp.eye(matrix.shape[0], dtype=matrix.dtype)
    return lax.linalg.triangular_solve(factor, unit_matrix, left_side=True, lower=True)

def component(start_flat, stiff_self, stiff_link, mass_self, coupling_blocks, interface_ids):
    dof_count, mode_count = start_flat.shape
    blocks_count = stiff_self.shape[0]
    block_size = stiff_self.shape[1]
    basis = start_flat
    stiff_basis = stiff_apply(stiff_self, stiff_link, basis.reshape(blocks_count, block_size, mode_count)).reshape(dof_count, mode_count)
    reduced = jnp.zeros((mode_count, mode_count), start_flat.dtype)
    for sweep in range(ITERS):
        filtered = basis - step_size * stiff_basis
        mass_part = block_product(mass_self, filtered.reshape(blocks_count, block_size, mode_count)).reshape(dof_count, mode_count)
        mass_gram = jnp.dot(filtered.T, mass_part, precision=highest) / dof_count
        factor_inv = lower_inverse(mass_gram)
        basis = jnp.dot(filtered, factor_inv.T, precision=highest)
        stiff_basis = stiff_apply(stiff_self, stiff_link, basis.reshape(blocks_count, block_size, mode_count)).reshape(dof_count, mode_count)
        reduced = jnp.dot(basis.T, stiff_basis, precision=highest) / dof_count
    block_terms = jnp.einsum('bkm,bkl->bml', basis.reshape(blocks_count, block_size, mode_count), coupling_blocks, precision=highest)
    onehot = (interface_ids[:, None] == jnp.arange(NIF, dtype=jnp.int32)[None, :]).astype(start_flat.dtype)
    coupling_proj = jnp.einsum('bj,bml->mjl', onehot, block_terms, precision=highest) / dof_count ** 0.5
    reduced_inv = lower_inverse(reduced)
    scaled = jnp.einsum('nm,mjl->njl', reduced_inv, coupling_proj, precision=highest)
    condensed = jnp.einsum('njk,njl->jkl', scaled, scaled, precision=highest)
    return (basis, reduced, condensed)

def reference(start_modes, stiff_diag, stiff_off, mass_blocks, coupling, interface_block, global_iface):
    modes, reduced, condensed = lax.map(lambda packed: component(*packed), (start_modes, stiff_diag, stiff_off, mass_blocks, coupling, interface_block))
    placed = (global_iface[:, :, None] == jnp.arange(GIF, dtype=jnp.int32)[None, None, :]).astype(start_modes.dtype)
    assembled = jnp.einsum('cjg,cjkl->gkl', placed, condensed, precision=highest)
    return (modes, reduced, assembled)
```

```python
import functools

import jax
import jax.numpy as jnp
from jax import lax
from jax.experimental import pallas as pl
from jax.experimental.pallas import tpu as pltpu
from jax.sharding import PartitionSpec as P

BF = jnp.bfloat16
F32 = jnp.float32
STEP = 0.15
MESH = pl.DeviceIdType.MESH
HI = lax.Precision.HIGHEST
MIB = 1 << 20


def split(x):
    hi = x.astype(BF)
    lo = (x - hi.astype(F32)).astype(BF)
    return hi, lo


def mm(a, b):
    return jnp.dot(a, b, preferred_element_type=F32)


def mmh(a, b):
    return jnp.dot(a, b, preferred_element_type=F32, precision=HI)


def chain_kernel(nb, count, x_ref, d_ref, e_ref, yh_ref, yl_ref, zh_ref, zl_ref,
                 xh, xl, fh, fl, eyh, eyl, ah, al, edge, halo, enext, send_sem, recv_sem):
    pairs = nb // 2
    rows = nb * 128
    me = lax.axis_index("blk")
    left, right = lax.rem(me + count - 1, count), lax.rem(me + 1, count)
    barrier = pltpu.get_barrier_semaphore()
    for peer in (left, right):
        pl.semaphore_signal(barrier, inc=1, device_id={"blk": peer}, device_id_type=MESH)
    pl.semaphore_wait(barrier, 2)

    def send(src, dst, slot, peer):
        copy = pltpu.make_async_remote_copy(
            src_ref=src, dst_ref=dst, send_sem=send_sem.at[slot], recv_sem=recv_sem.at[slot],
            device_id={"blk": peer}, device_id_type=MESH)
        copy.start()
        return copy

    copies = [
        send(e_ref.at[0], enext, 6, left),
        send(x_ref.at[pl.ds(rows - 128, 128)], halo.at[0], 0, right),
        send(x_ref.at[pl.ds(0, 128)], halo.at[1], 1, left),
    ]
    has_left = me > 0
    has_right = me < count - 1

    def put_a(p, row, col, block):
        hi, lo = split(block)
        ah[p, row * 128:(row + 1) * 128, col * 128:(col + 1) * 128] = hi
        al[p, row * 128:(row + 1) * 128, col * 128:(col + 1) * 128] = lo

    zero = jnp.zeros((128, 128), F32)

    def build(p, _):
        b = 2 * p
        e0 = e_ref[b]
        e0 = jnp.where(jnp.logical_or(has_left, p > 0), e0, 0.0)
        e1 = e_ref[b + 1]
        put_a(p, 0, 0, e0)
        put_a(p, 0, 1, d_ref[b])
        put_a(p, 0, 2, e1.T)
        put_a(p, 0, 3, zero)
        put_a(p, 1, 0, zero)
        put_a(p, 1, 1, e1)
        put_a(p, 1, 2, d_ref[b + 1])
        e2 = e_ref[jnp.minimum(b + 2, nb - 1)]
        put_a(p, 1, 3, e2.T)
        r = pl.multiple_of(p * 256, 256)
        hi, lo = split(x_ref[pl.ds(r, 256), :])
        o = pl.multiple_of(r + 128, 128)
        xh[pl.ds(o, 256), :] = hi
        xl[pl.ds(o, 256), :] = lo
        return 0

    lax.fori_loop(0, pairs, build, 0)

    def product(vh, vl, p):
        r = pl.multiple_of(p * 256, 256)
        h = vh[pl.ds(r, 512), :]
        l = vl[pl.ds(r, 512), :]
        a = ah[p]
        return mm(a, h) + mm(a, l) + mm(al[p], h)

    def own(p):
        return pl.ds(pl.multiple_of(p * 256 + 128, 128), 256)

    def apply_f(p):
        acc = product(xh, xl, p)
        x = x_ref[pl.ds(pl.multiple_of(p * 256, 256), 256), :]
        f = x * (1.0 / 256) - acc * (STEP / 256)
        hi, lo = split(f)
        fh[own(p), :] = hi
        fl[own(p), :] = lo
        return f

    def apply_y(p):
        acc = product(fh, fl, p)
        f = fh[own(p), :].astype(F32) + fl[own(p), :].astype(F32)
        y = f - acc * STEP
        hi, lo = split(y)
        eyh[own(p), :] = hi
        eyl[own(p), :] = lo
        o = pl.ds(pl.multiple_of(p * 256, 256), 256)
        yh_ref[o, :] = hi
        yl_ref[o, :] = lo
        return y

    def apply_z(p):
        acc = product(eyh, eyl, p)
        hi, lo = split(acc)
        o = pl.ds(pl.multiple_of(p * 256, 256), 256)
        zh_ref[o, :] = hi
        zl_ref[o, :] = lo
        return acc

    for rnd, (fn, vh, vl) in enumerate(((apply_f, xh, xl), (apply_y, fh, fl), (apply_z, eyh, eyl))):
        def body(p, _, fn=fn):
            fn(p)
            return 0

        lax.fori_loop(1, pairs - 1, body, 0)
        if rnd == 0:
            copies[0].wait()
            e2 = jnp.where(has_right, enext[...], 0.0)
            put_a(pairs - 1, 1, 3, e2.T)
        copies[2 * rnd + 1].wait()
        hi, lo = split(jnp.where(has_left, halo[2 * rnd], 0.0))
        vh[0:128, :] = hi
        vl[0:128, :] = lo
        copies[2 * rnd + 2].wait()
        hi, lo = split(jnp.where(has_right, halo[2 * rnd + 1], 0.0))
        vh[rows + 128:rows + 256, :] = hi
        vl[rows + 128:rows + 256, :] = lo
        last = fn(pairs - 1)
        if rnd < 2:
            edge[2 * rnd] = last[128:, :]
            copies.append(send(edge.at[2 * rnd], halo.at[2 * rnd + 2], 2 * rnd + 2, right))
        first = fn(0)
        if rnd < 2:
            edge[2 * rnd + 1] = first[:128, :]
            copies.append(send(edge.at[2 * rnd + 1], halo.at[2 * rnd + 3], 2 * rnd + 3, left))


def chain(x, d, e, count):
    nb = d.shape[0]
    rows = nb * 128
    ext = pltpu.VMEM((rows + 256, 256), BF)
    vm = pl.BlockSpec(memory_space=pltpu.VMEM)
    out = jax.ShapeDtypeStruct((rows, 256), BF)
    return pl.pallas_call(
        functools.partial(chain_kernel, nb, count),
        out_shape=(out,) * 4,
        in_specs=[vm] * 3,
        out_specs=(vm,) * 4,
        scratch_shapes=[ext] * 6 + [
            pltpu.VMEM((nb // 2, 256, 512), BF),
            pltpu.VMEM((nb // 2, 256, 512), BF),
            pltpu.VMEM((4, 128, 256), F32),
            pltpu.VMEM((6, 128, 256), F32),
            pltpu.VMEM((128, 128), F32),
            pltpu.SemaphoreType.DMA((7,)),
            pltpu.SemaphoreType.DMA((7,)),
        ],
        compiler_params=pltpu.CompilerParams(
            collective_id=0, has_side_effects=True, vmem_limit_bytes=60 * MIB),
        name="chain",
    )(x, d, e)


def gram_kernel(ids, yh_ref, yl_ref, zh_ref, zl_ref, m_ref, c_ref, ps_ref, w_ref):
    p = pl.program_id(0)

    @pl.when(p == 0)
    def _():
        ps_ref[...] = jnp.zeros_like(ps_ref)
        w_ref[...] = jnp.zeros_like(w_ref)

    yh, yl = yh_ref[...], yl_ref[...]
    parts = []
    for q in range(2):
        mh, ml = split(m_ref[q])
        left = jnp.concatenate(
            [jnp.concatenate([mh, mh], 1), jnp.concatenate([ml, ml], 1)], 0)
        s = slice(q * 128, (q + 1) * 128)
        both = mm(left, jnp.concatenate([yh[s], yl[s]], 0))
        parts.append(both[:128] + both[128:])
    myh, myl = split(jnp.concatenate(parts, 0))
    yth, ytl = yh.T, yl.T
    hi = jnp.concatenate([myh, zh_ref[...]], 1)
    lo = jnp.concatenate([myl, zl_ref[...]], 1)
    ps_ref[...] += mm(yth, hi) + mm(yth, lo) + mm(ytl, hi)
    for q in range(2):
        ch, cl = split(c_ref[q])
        cc = jnp.concatenate([ch, cl], 1)
        s = slice(q * 128, (q + 1) * 128)
        both = mm(jnp.concatenate([yth[:, s], ytl[:, s]], 1), jnp.concatenate([cc, cc], 0))
        j = ids[2 * p + q]
        term = jnp.where(j < 16, both[:, :128] + both[:, 128:], 0.0)
        slot = jnp.minimum(j, 15)
        w_ref[slot] = w_ref[slot] + term


def gram(ids, yh, yl, zh, zl, m, c):
    nb = m.shape[0]
    tile = pl.BlockSpec((256, 256), lambda p, ids: (p, 0))
    blocks = pl.BlockSpec((2, 128, 128), lambda p, ids: (p, 0, 0))
    return pl.pallas_call(
        gram_kernel,
        out_shape=(jax.ShapeDtypeStruct((256, 512), F32), jax.ShapeDtypeStruct((16, 256, 128), F32)),
        grid_spec=pltpu.PrefetchScalarGridSpec(
            num_scalar_prefetch=1,
            grid=(nb // 2,),
            in_specs=[tile] * 4 + [blocks] * 2,
            out_specs=(pl.BlockSpec((256, 512), lambda p, ids: (0, 0)),
                       pl.BlockSpec((16, 256, 128), lambda p, ids: (0, 0, 0))),
        ),
        compiler_params=pltpu.CompilerParams(vmem_limit_bytes=40 * MIB),
        name="gram",
    )(ids, yh, yl, zh, zl, m, c)


def diag_inverse(mats):
    size = 64
    groups = size // 8
    sub = lax.broadcasted_iota(jnp.int32, (8, 128), 0)
    lane = lax.broadcasted_iota(jnp.int32, (8, 128), 1)
    state = []
    for mat in mats:
        full = jnp.concatenate([mat, jnp.zeros_like(mat)], 1)
        state.append([
            jnp.where(lane == sub + (64 + 8 * g), 1.0, full[8 * g:8 * g + 8]) for g in range(groups)
        ])
    for k in range(groups):
        cols = [[[jnp.broadcast_to(rows[g][:, 8 * k + c:8 * k + c + 1], (8, 128)) for c in range(8)]
                 for g in range(k, groups)] for rows in state]
        for c in range(8):
            for rows, col in zip(state, cols):
                mine = col[0]
                rs = lax.rsqrt(jnp.broadcast_to(mine[c][c:c + 1, :], (8, 128)))
                u = jnp.broadcast_to(rows[k][c:c + 1, :], (8, 128)) * rs
                heads = {n: jnp.broadcast_to(mine[n][c:c + 1, :], (8, 128)) * rs for n in range(c + 1, 8)}
                for g in range(k, groups):
                    mult = col[g - k][c] * rs
                    if g == k:
                        mult = jnp.where(sub > c, mult, 0.0)
                        rows[g] = jnp.where(sub == c, u, rows[g] - mult * u)
                    else:
                        rows[g] = rows[g] - mult * u
                    for n in range(c + 1, 8):
                        col[g - k][n] = col[g - k][n] - mult * heads[n]
    return [jnp.concatenate(rows, 0) for rows in state]


def factor_kernel(ps_ref, cth_ref, ctl_ref, red_ref, qi_ref, a_ref, x_ref):
    size = 256
    row = lax.broadcasted_iota(jnp.int32, (size, size), 0)
    column = lax.broadcasted_iota(jnp.int32, (size, size), 1)
    for t in range(2):
        g = ps_ref[:, t * size:(t + 1) * size]
        a_ref[t] = (g + g.T) * 0.5
        x_ref[t] = jnp.where(row == column, 1.0, 0.0)
    for k in range(4):
        lo, hi = 64 * k, 64 * (k + 1)
        inv = diag_inverse([a_ref[t, lo:hi, lo:hi] for t in range(2)])
        for t in range(2):
            tri = inv[t][:, 64:]
            xu = mmh(tri, x_ref[t, lo:hi, :])
            x_ref[t, lo:hi, :] = xu
            if k < 3:
                au = mmh(tri, a_ref[t, lo:hi, :])
                low = au[:, hi:].T
                a_ref[t, hi:, :] = a_ref[t, hi:, :] - mmh(low, au)
                x_ref[t, hi:, :] = x_ref[t, hi:, :] - mmh(low, xu)
    ci = x_ref[0]
    ct = ci.T
    red_ref[...] = mmh(mmh(ci, ps_ref[:, size:]), ct)
    qi_ref[...] = x_ref[1]
    h, l = split(ct * 256.0)
    cth_ref[...] = h
    ctl_ref[...] = l


def factor(ps):
    sq = jax.ShapeDtypeStruct((256, 256), F32)
    sb = jax.ShapeDtypeStruct((256, 256), BF)
    vm = pl.BlockSpec(memory_space=pltpu.VMEM)
    return pl.pallas_call(
        factor_kernel,
        out_shape=(sb, sb, sq, sq),
        in_specs=[vm],
        out_specs=(vm,) * 4,
        scratch_shapes=[pltpu.VMEM((2, 256, 256), F32)] * 2,
        compiler_params=pltpu.CompilerParams(vmem_limit_bytes=32 * MIB),
        cost_estimate=pl.CostEstimate(flops=4 * 10**9, bytes_accessed=10**6, transcendentals=0),
        name="factor",
    )(ps)


def modes_kernel(yh_ref, yl_ref, cth_ref, ctl_ref, out_ref):
    h = yh_ref[...]
    out_ref[...] = mm(h, cth_ref[...]) + mm(h, ctl_ref[...]) + mm(yl_ref[...], cth_ref[...])


def modes_of(yh, yl, cth, ctl):
    rows = yh.shape[0]
    t = 512
    tile = pl.BlockSpec((t, 256), lambda p: (p, 0))
    whole = pl.BlockSpec((256, 256), lambda p: (0, 0))
    return pl.pallas_call(
        modes_kernel,
        out_shape=jax.ShapeDtypeStruct((rows, 256), F32),
        grid=(rows // t,),
        in_specs=[tile, tile, whole, whole],
        out_specs=tile,
        name="modes",
    )(yh, yl, cth, ctl)


def condense_kernel(qi_ref, w_ref, out_ref):
    scaled = mmh(qi_ref[...], w_ref[...])
    out_ref[...] = mmh(scaled.T, scaled)


def condense(qi, w):
    vm = pl.BlockSpec(memory_space=pltpu.VMEM)
    return pl.pallas_call(
        condense_kernel,
        out_shape=jax.ShapeDtypeStruct((128, 128), F32),
        in_specs=[vm] * 2,
        out_specs=vm,
        name="condense",
    )(qi, w)


def local(start_modes, stiff_diag, stiff_off, mass_blocks, coupling, interface_block, global_iface):
    count = lax.axis_size("blk")
    yh, yl, zh, zl = chain(start_modes[0], stiff_diag[0], stiff_off[0], count)
    ps, w = gram(interface_block[0], yh, yl, zh, zl, mass_blocks[0], coupling[0])
    ps = lax.psum(ps, "blk")
    mine = lax.psum_scatter(w, "blk", scatter_dimension=0, tiled=False)
    cth, ctl, reduced, qi = factor(ps)
    modes = modes_of(yh, yl, cth, ctl)
    cond = condense(qi, mine)
    pieces = lax.all_to_all(cond.reshape(count, 128 // count, 128), "blk", 0, 0, tiled=True)
    owners = lax.axis_size("comp")
    hot = (jnp.arange(4 * owners, dtype=jnp.int32)[:, None] == global_iface[0][None, :]).astype(F32)
    dense = jnp.einsum("gj,jkl->gkl", hot, pieces, precision=HI)
    slab = jnp.sum(lax.all_to_all(dense.reshape(owners, 4, 128 // count, 128), "comp", 0, 0, tiled=True), 0)
    assembled = lax.all_gather(slab, "blk", axis=1, tiled=True)
    return modes[None], reduced[None], assembled


def solution(mesh):
    in_specs = (
        P("comp", "blk", None),
        P("comp", "blk", None, None),
        P("comp", "blk", None, None),
        P("comp", "blk", None, None),
        P("comp", "blk", None, None),
        P("comp", "blk"),
        P("comp", None),
    )
    out_specs = (P("comp", "blk", None), P("comp", None, None), P("comp", None, None))
    return jax.shard_map(local, mesh=mesh, in_specs=in_specs, out_specs=out_specs, check_vma=False)
```

```python
import functools

import jax
import jax.numpy as jnp
from jax import lax
from jax.experimental import pallas as pl
from jax.experimental.pallas import tpu as pltpu
from jax.sharding import PartitionSpec as P

BF = jnp.bfloat16
F32 = jnp.float32
STEP = 0.15
MESH = pl.DeviceIdType.MESH
HI = lax.Precision.HIGHEST
MIB = 1 << 20


def split(x):
    hi = x.astype(BF)
    lo = (x - hi.astype(F32)).astype(BF)
    return hi, lo


def mm(a, b):
    return jnp.dot(a, b, preferred_element_type=F32)


def mmh(a, b):
    return jnp.dot(a, b, preferred_element_type=F32, precision=HI)


def chain_kernel(nb, count, x_ref, d_ref, e_ref, yh_ref, yl_ref, zh_ref, zl_ref,
                 xh, xl, fh, fl, eyh, eyl, ah, al, edge, halo, enext, send_sem, recv_sem):
    pairs = nb // 2
    rows = nb * 128
    me = lax.axis_index("blk")
    left, right = lax.rem(me + count - 1, count), lax.rem(me + 1, count)
    barrier = pltpu.get_barrier_semaphore()
    for peer in (left, right):
        pl.semaphore_signal(barrier, inc=1, device_id={"blk": peer}, device_id_type=MESH)
    pl.semaphore_wait(barrier, 2)

    def send(src, dst, slot, peer):
        copy = pltpu.make_async_remote_copy(
            src_ref=src, dst_ref=dst, send_sem=send_sem.at[slot], recv_sem=recv_sem.at[slot],
            device_id={"blk": peer}, device_id_type=MESH)
        copy.start()
        return copy

    copies = [
        send(e_ref.at[0], enext, 6, left),
        send(x_ref.at[pl.ds(rows - 128, 128)], halo.at[0], 0, right),
        send(x_ref.at[pl.ds(0, 128)], halo.at[1], 1, left),
    ]
    has_left = me > 0
    has_right = me < count - 1

    def put_a(p, row, col, block):
        hi, lo = split(block)
        ah[p, row * 128:(row + 1) * 128, col * 128:(col + 1) * 128] = hi
        al[p, row * 128:(row + 1) * 128, col * 128:(col + 1) * 128] = lo

    zero = jnp.zeros((128, 128), F32)

    def build(p, _):
        b = 2 * p
        e0 = e_ref[b]
        e0 = jnp.where(jnp.logical_or(has_left, p > 0), e0, 0.0)
        e1 = e_ref[b + 1]
        put_a(p, 0, 0, e0)
        put_a(p, 0, 1, d_ref[b])
        put_a(p, 0, 2, e1.T)
        put_a(p, 0, 3, zero)
        put_a(p, 1, 0, zero)
        put_a(p, 1, 1, e1)
        put_a(p, 1, 2, d_ref[b + 1])
        e2 = e_ref[jnp.minimum(b + 2, nb - 1)]
        put_a(p, 1, 3, e2.T)
        r = pl.multiple_of(p * 256, 256)
        hi, lo = split(x_ref[pl.ds(r, 256), :])
        o = pl.multiple_of(r + 128, 128)
        xh[pl.ds(o, 256), :] = hi
        xl[pl.ds(o, 256), :] = lo
        return 0

    lax.fori_loop(0, pairs, build, 0)

    def product(vh, vl, p):
        r = pl.multiple_of(p * 256, 256)
        h = vh[pl.ds(r, 512), :]
        l = vl[pl.ds(r, 512), :]
        a = ah[p]
        return mm(a, h) + mm(a, l) + mm(al[p], h)

    def own(p):
        return pl.ds(pl.multiple_of(p * 256 + 128, 128), 256)

    def apply_f(p):
        acc = product(xh, xl, p)
        x = x_ref[pl.ds(pl.multiple_of(p * 256, 256), 256), :]
        f = x * (1.0 / 256) - acc * (STEP / 256)
        hi, lo = split(f)
        fh[own(p), :] = hi
        fl[own(p), :] = lo
        return f

    def apply_y(p):
        acc = product(fh, fl, p)
        f = fh[own(p), :].astype(F32) + fl[own(p), :].astype(F32)
        y = f - acc * STEP
        hi, lo = split(y)
        eyh[own(p), :] = hi
        eyl[own(p), :] = lo
        o = pl.ds(pl.multiple_of(p * 256, 256), 256)
        yh_ref[o, :] = hi
        yl_ref[o, :] = lo
        return y

    def apply_z(p):
        acc = product(eyh, eyl, p)
        hi, lo = split(acc)
        o = pl.ds(pl.multiple_of(p * 256, 256), 256)
        zh_ref[o, :] = hi
        zl_ref[o, :] = lo
        return acc

    for rnd, (fn, vh, vl) in enumerate(((apply_f, xh, xl), (apply_y, fh, fl), (apply_z, eyh, eyl))):
        def body(p, _, fn=fn):
            fn(p)
            return 0

        lax.fori_loop(1, pairs - 1, body, 0)
        if rnd == 0:
            copies[0].wait()
            e2 = jnp.where(has_right, enext[...], 0.0)
            put_a(pairs - 1, 1, 3, e2.T)
        copies[2 * rnd + 1].wait()
        hi, lo = split(jnp.where(has_left, halo[2 * rnd], 0.0))
        vh[0:128, :] = hi
        vl[0:128, :] = lo
        copies[2 * rnd + 2].wait()
        hi, lo = split(jnp.where(has_right, halo[2 * rnd + 1], 0.0))
        vh[rows + 128:rows + 256, :] = hi
        vl[rows + 128:rows + 256, :] = lo
        last = fn(pairs - 1)
        if rnd < 2:
            edge[2 * rnd] = last[128:, :]
            copies.append(send(edge.at[2 * rnd], halo.at[2 * rnd + 2], 2 * rnd + 2, right))
        first = fn(0)
        if rnd < 2:
            edge[2 * rnd + 1] = first[:128, :]
            copies.append(send(edge.at[2 * rnd + 1], halo.at[2 * rnd + 3], 2 * rnd + 3, left))


def chain(x, d, e, count):
    nb = d.shape[0]
    rows = nb * 128
    ext = pltpu.VMEM((rows + 256, 256), BF)
    vm = pl.BlockSpec(memory_space=pltpu.VMEM)
    out = jax.ShapeDtypeStruct((rows, 256), BF)
    return pl.pallas_call(
        functools.partial(chain_kernel, nb, count),
        out_shape=(out,) * 4,
        in_specs=[vm] * 3,
        out_specs=(vm,) * 4,
        scratch_shapes=[ext] * 6 + [
            pltpu.VMEM((nb // 2, 256, 512), BF),
            pltpu.VMEM((nb // 2, 256, 512), BF),
            pltpu.VMEM((4, 128, 256), F32),
            pltpu.VMEM((6, 128, 256), F32),
            pltpu.VMEM((128, 128), F32),
            pltpu.SemaphoreType.DMA((7,)),
            pltpu.SemaphoreType.DMA((7,)),
        ],
        compiler_params=pltpu.CompilerParams(
            collective_id=0, has_side_effects=True, vmem_limit_bytes=60 * MIB),
        name="chain",
    )(x, d, e)


def gram_kernel(ids, yh_ref, yl_ref, zh_ref, zl_ref, m_ref, c_ref, ps_ref, w_ref):
    p = pl.program_id(0)

    @pl.when(p == 0)
    def _():
        ps_ref[...] = jnp.zeros_like(ps_ref)
        w_ref[...] = jnp.zeros_like(w_ref)

    yh, yl = yh_ref[...], yl_ref[...]
    parts = []
    for q in range(2):
        mh, ml = split(m_ref[q])
        left = jnp.concatenate(
            [jnp.concatenate([mh, mh], 1), jnp.concatenate([ml, ml], 1)], 0)
        s = slice(q * 128, (q + 1) * 128)
        both = mm(left, jnp.concatenate([yh[s], yl[s]], 0))
        parts.append(both[:128] + both[128:])
    myh, myl = split(jnp.concatenate(parts, 0))
    yth, ytl = yh.T, yl.T
    hi = jnp.concatenate([myh, zh_ref[...]], 1)
    lo = jnp.concatenate([myl, zl_ref[...]], 1)
    ps_ref[...] += mm(yth, hi) + mm(yth, lo) + mm(ytl, hi)
    for q in range(2):
        ch, cl = split(c_ref[q])
        cc = jnp.concatenate([ch, cl], 1)
        s = slice(q * 128, (q + 1) * 128)
        both = mm(jnp.concatenate([yth[:, s], ytl[:, s]], 1), jnp.concatenate([cc, cc], 0))
        j = ids[2 * p + q]
        term = jnp.where(j < 16, both[:, :128] + both[:, 128:], 0.0)
        slot = jnp.minimum(j, 15)
        w_ref[slot] = w_ref[slot] + term


def gram(ids, yh, yl, zh, zl, m, c):
    nb = m.shape[0]
    tile = pl.BlockSpec((256, 256), lambda p, ids: (p, 0))
    blocks = pl.BlockSpec((2, 128, 128), lambda p, ids: (p, 0, 0))
    return pl.pallas_call(
        gram_kernel,
        out_shape=(jax.ShapeDtypeStruct((256, 512), F32), jax.ShapeDtypeStruct((16, 256, 128), F32)),
        grid_spec=pltpu.PrefetchScalarGridSpec(
            num_scalar_prefetch=1,
            grid=(nb // 2,),
            in_specs=[tile] * 4 + [blocks] * 2,
            out_specs=(pl.BlockSpec((256, 512), lambda p, ids: (0, 0)),
                       pl.BlockSpec((16, 256, 128), lambda p, ids: (0, 0, 0))),
        ),
        compiler_params=pltpu.CompilerParams(vmem_limit_bytes=40 * MIB),
        name="gram",
    )(ids, yh, yl, zh, zl, m, c)


def diag_inverse(mats):
    size = 64
    groups = size // 8
    sub = lax.broadcasted_iota(jnp.int32, (8, 128), 0)
    lane = lax.broadcasted_iota(jnp.int32, (8, 128), 1)
    state = []
    for mat in mats:
        full = jnp.concatenate([mat, jnp.zeros_like(mat)], 1)
        state.append([
            jnp.where(lane == sub + (64 + 8 * g), 1.0, full[8 * g:8 * g + 8]) for g in range(groups)
        ])
    for k in range(groups):
        cols = [[[jnp.broadcast_to(rows[g][:, 8 * k + c:8 * k + c + 1], (8, 128)) for c in range(8)]
                 for g in range(k, groups)] for rows in state]
        for c in range(8):
            for rows, col in zip(state, cols):
                mine = col[0]
                rs = lax.rsqrt(jnp.broadcast_to(mine[c][c:c + 1, :], (8, 128)))
                u = jnp.broadcast_to(rows[k][c:c + 1, :], (8, 128)) * rs
                heads = {n: jnp.broadcast_to(mine[n][c:c + 1, :], (8, 128)) * rs for n in range(c + 1, 8)}
                for g in range(k, groups):
                    mult = col[g - k][c] * rs
                    if g == k:
                        mult = jnp.where(sub > c, mult, 0.0)
                        rows[g] = jnp.where(sub == c, u, rows[g] - mult * u)
                    else:
                        rows[g] = rows[g] - mult * u
                    for n in range(c + 1, 8):
                        col[g - k][n] = col[g - k][n] - mult * heads[n]
    return [jnp.concatenate(rows, 0) for rows in state]


def modes_kernel(yh_ref, yl_ref, cth_ref, ctl_ref, out_ref):
    h = yh_ref[...]
    out_ref[...] = mm(h, cth_ref[...]) + mm(h, ctl_ref[...]) + mm(yl_ref[...], cth_ref[...])


def modes_of(yh, yl, cth, ctl):
    rows = yh.shape[0]
    t = 512
    tile = pl.BlockSpec((t, 256), lambda p: (p, 0))
    whole = pl.BlockSpec((256, 256), lambda p: (0, 0))
    return pl.pallas_call(
        modes_kernel,
        out_shape=jax.ShapeDtypeStruct((rows, 256), F32),
        grid=(rows // t,),
        in_specs=[tile, tile, whole, whole],
        out_specs=tile,
        name="modes",
    )(yh, yl, cth, ctl)


EARLY = 5


def offsets(me):
    y, z = me // 4, lax.rem(me, 4)
    turns = ((0, 1), (1, 0), (0, 3), (3, 0), (1, 1), (3, 3), (1, 3), (3, 1),
             (0, 2), (2, 0), (1, 2), (2, 1), (3, 2), (2, 3), (2, 2))
    return [lax.rem(y + dy, 4) * 4 + lax.rem(z + dz, 4) for dy, dz in turns]


def finish_kernel(owners, ps_ref, w_ref, hot_ref, cth_ref, ctl_ref, red_ref, asm_ref,
                  ps_in, ps_all, w_in, a_ref, x_ref, cond_ref, cond_in, dense, dense_in, slab,
                  slab_in, send_sem, recv_sem):
    count = 16
    size = 256
    me = lax.axis_index("blk")
    mine = lax.axis_index("comp")
    peers = offsets(me)
    friends = [lax.rem(mine + d, owners) for d in range(1, owners)]
    barrier = pltpu.get_barrier_semaphore()
    for p in peers:
        pl.semaphore_signal(barrier, inc=1, device_id={"blk": p}, device_id_type=MESH)
    for f in friends:
        pl.semaphore_signal(barrier, inc=1, device_id={"comp": f}, device_id_type=MESH)
    pl.semaphore_wait(barrier, len(peers) + len(friends))

    def copy(src, dst, phase, peer, slot, axis="blk"):
        return pltpu.make_async_remote_copy(
            src_ref=src, dst_ref=dst, send_sem=send_sem.at[phase, peer],
            recv_sem=recv_sem.at[phase, slot], device_id={axis: peer}, device_id_type=MESH)

    def part(p):
        return pl.ds(pl.multiple_of(p * 16, 16), 16)

    gram_out = [copy(ps_ref.at[part(p)], ps_in.at[me], 0, p, me) for p in peers]
    w_out = [copy(w_ref.at[p], w_in.at[me], 2, p, me) for p in peers]
    for c in gram_out:
        c.start()
    for c in w_out[:EARLY]:
        c.start()
    acc = ps_ref[part(me), :]
    for p in peers:
        copy(ps_ref.at[part(p)], ps_in.at[p], 0, p, p).wait_recv()
        acc = acc + ps_in[p]
    ps_all[part(me), :] = acc
    own = ps_all.at[part(me)]
    sums_out = [copy(own, own, 1, p, me) for p in peers]
    for c in sums_out:
        c.start()
    for c in w_out[EARLY:]:
        c.start()
    for p in peers:
        copy(own, ps_all.at[part(p)], 1, p, p).wait_recv()

    row = lax.broadcasted_iota(jnp.int32, (size, size), 0)
    column = lax.broadcasted_iota(jnp.int32, (size, size), 1)
    for t in range(2):
        g = ps_all[:, t * size:(t + 1) * size]
        a_ref[t] = (g + g.T) * 0.5
        x_ref[t] = jnp.where(row == column, 1.0, 0.0)
    for k in range(4):
        lo, hi = 64 * k, 64 * (k + 1)
        inv = diag_inverse([a_ref[t, lo:hi, lo:hi] for t in range(2)])
        for t in range(2):
            tri = inv[t][:, 64:]
            xu = mmh(tri, x_ref[t, lo:hi, :])
            x_ref[t, lo:hi, :] = xu
            if k < 3:
                au = mmh(tri, a_ref[t, lo:hi, :])
                low = au[:, hi:].T
                a_ref[t, hi:, :] = a_ref[t, hi:, :] - mmh(low, au)
                x_ref[t, hi:, :] = x_ref[t, hi:, :] - mmh(low, xu)

    total = w_ref[me]
    for p in peers:
        copy(w_ref.at[p], w_in.at[p], 2, p, p).wait_recv()
        total = total + w_in[p]
    scaled = mmh(x_ref[1], total)
    cond_ref[...] = mmh(scaled.T, scaled)

    def eight(p):
        return pl.ds(pl.multiple_of(p * 8, 8), 8)

    cond_out = [copy(cond_ref.at[eight(p)], cond_in.at[me], 3, p, me) for p in peers]
    for c in cond_out:
        c.start()
    ci = x_ref[0]
    ct = ci.T
    red_ref[...] = mmh(mmh(ci, ps_all[:, size:]), ct)
    h, l = split(ct * 256.0)
    cth_ref[...] = h
    ctl_ref[...] = l
    cond_in[me] = cond_ref[eight(me), :]
    for p in peers:
        copy(cond_ref.at[eight(p)], cond_in.at[p], 3, p, p).wait_recv()
    pieces = [cond_in[i] for i in range(count)]
    for g in range(4 * owners):
        dense[g] = sum(hot_ref[g, i] * pieces[i] for i in range(count))

    def four(o):
        return pl.ds(o * 4, 4)

    dense_out = [copy(dense.at[four(f)], dense_in.at[mine], 4, f, mine, "comp") for f in friends]
    for c in dense_out:
        c.start()
    acc = dense[four(mine)]
    for f in friends:
        copy(dense.at[four(f)], dense_in.at[f], 4, f, f, "comp").wait_recv()
        acc = acc + dense_in[f]
    slab[...] = acc
    slab_out = [copy(slab, slab_in.at[me], 5, p, me) for p in peers]
    for c in slab_out:
        c.start()
    asm_ref[:, eight(me), :] = acc
    for p in peers:
        copy(slab, slab_in.at[p], 5, p, p).wait_recv()
        asm_ref[:, eight(p), :] = slab_in[p]
    for c in gram_out + w_out + sums_out + cond_out + dense_out + slab_out:
        c.wait_send()


def finish(ps, w, hot, owners):
    sq = jax.ShapeDtypeStruct((256, 256), F32)
    sb = jax.ShapeDtypeStruct((256, 256), BF)
    vm = pl.BlockSpec(memory_space=pltpu.VMEM)
    return pl.pallas_call(
        functools.partial(finish_kernel, owners),
        out_shape=(sb, sb, sq, jax.ShapeDtypeStruct((4, 128, 128), F32)),
        in_specs=[vm, vm, pl.BlockSpec(memory_space=pltpu.SMEM)],
        out_specs=(vm,) * 4,
        scratch_shapes=[
            pltpu.VMEM((16, 16, 512), F32),
            pltpu.VMEM((256, 512), F32),
            pltpu.VMEM((16, 256, 128), F32),
            pltpu.VMEM((2, 256, 256), F32),
            pltpu.VMEM((2, 256, 256), F32),
            pltpu.VMEM((128, 128), F32),
            pltpu.VMEM((16, 8, 128), F32),
            pltpu.VMEM((4 * owners, 8, 128), F32),
            pltpu.VMEM((owners, 4, 8, 128), F32),
            pltpu.VMEM((4, 8, 128), F32),
            pltpu.VMEM((16, 4, 8, 128), F32),
            pltpu.SemaphoreType.DMA((6, 16)),
            pltpu.SemaphoreType.DMA((6, 16)),
        ],
        compiler_params=pltpu.CompilerParams(
            collective_id=1, has_side_effects=True, vmem_limit_bytes=40 * MIB),
        name="finish",
    )(ps, w, hot)


def local(start_modes, stiff_diag, stiff_off, mass_blocks, coupling, interface_block, global_iface):
    owners = lax.axis_size("comp")
    yh, yl, zh, zl = chain(start_modes[0], stiff_diag[0], stiff_off[0], lax.axis_size("blk"))
    ps, w = gram(interface_block[0], yh, yl, zh, zl, mass_blocks[0], coupling[0])
    hot = (jnp.arange(4 * owners, dtype=jnp.int32)[:, None] == global_iface[0][None, :]).astype(F32)
    cth, ctl, reduced, assembled = finish(ps, w, hot, owners)
    modes = modes_of(yh, yl, cth, ctl)
    return modes[None], reduced[None], assembled


def solution(mesh):
    in_specs = (
        P("comp", "blk", None),
        P("comp", "blk", None, None),
        P("comp", "blk", None, None),
        P("comp", "blk", None, None),
        P("comp", "blk", None, None),
        P("comp", "blk"),
        P("comp", None),
    )
    out_specs = (P("comp", "blk", None), P("comp", None, None), P("comp", None, None))
    return jax.shard_map(local, mesh=mesh, in_specs=in_specs, out_specs=out_specs, check_vma=False)
```

```python
import functools

import jax
import jax.numpy as jnp
from jax import lax
from jax.experimental import pallas as pl
from jax.experimental.pallas import tpu as pltpu
from jax.sharding import PartitionSpec as P

BF = jnp.bfloat16
F32 = jnp.float32
STEP = 0.15
MESH = pl.DeviceIdType.MESH
HI = lax.Precision.HIGHEST
MIB = 1 << 20
NB = 32
ROWS = NB * 128
BLK = 16
COMP = 8
CHUNKS = 4
EARLY = 6


def split(x):
    hi = x.astype(BF)
    lo = (x - hi.astype(F32)).astype(BF)
    return hi, lo


def mm(a, b):
    return jnp.dot(a, b, preferred_element_type=F32)


def mmh(a, b):
    return jnp.dot(a, b, preferred_element_type=F32, precision=HI)


def cat(parts, axis):
    return jnp.concatenate(parts, axis)


def rows_at(start, size):
    return pl.ds(pl.multiple_of(start, min(size, 128)), size)


def diag_inverse(mats):
    groups = 8
    sub = lax.broadcasted_iota(jnp.int32, (8, 128), 0)
    lane = lax.broadcasted_iota(jnp.int32, (8, 128), 1)
    state = []
    for mat in mats:
        full = cat([mat, jnp.zeros_like(mat)], 1)
        state.append([
            jnp.where(lane == sub + (64 + 8 * g), 1.0, full[8 * g:8 * g + 8]) for g in range(groups)
        ])
    for k in range(groups):
        cols = [[[jnp.broadcast_to(rows[g][:, 8 * k + c:8 * k + c + 1], (8, 128)) for c in range(8)]
                 for g in range(k, groups)] for rows in state]
        for c in range(8):
            for rows, col in zip(state, cols):
                mine = col[0]
                rs = lax.rsqrt(jnp.broadcast_to(mine[c][c:c + 1, :], (8, 128)))
                u = jnp.broadcast_to(rows[k][c:c + 1, :], (8, 128)) * rs
                heads = {n: jnp.broadcast_to(mine[n][c:c + 1, :], (8, 128)) * rs for n in range(c + 1, 8)}
                for g in range(k, groups):
                    mult = col[g - k][c] * rs
                    if g == k:
                        mult = jnp.where(sub > c, mult, 0.0)
                        rows[g] = jnp.where(sub == c, u, rows[g] - mult * u)
                    else:
                        rows[g] = rows[g] - mult * u
                    for n in range(c + 1, 8):
                        col[g - k][n] = col[g - k][n] - mult * heads[n]
    return [cat(rows, 0) for rows in state]


def offsets(me):
    y, z = me // 4, lax.rem(me, 4)
    turns = ((0, 1), (1, 0), (0, 3), (3, 0), (1, 1), (3, 3), (1, 3), (3, 1),
             (0, 2), (2, 0), (1, 2), (2, 1), (3, 2), (2, 3), (2, 2))
    return [lax.rem(y + dy, 4) * 4 + lax.rem(z + dz, 4) for dy, dz in turns]


def kernel(links, hot, x_hbm, d_hbm, e_hbm, m_hbm, c_hbm, modes_ref, red_ref, asm_ref,
           x, d, e, m, cpl, xh, xl, fh, fl, yh, yl, ah, al, cum, ct,
           edge, halo, enext, gram, gram_in, sums, w, w_in, fa, fx,
           cond, cond_in, dense, dense_in, slab, slab_in,
           load_sem, halo_send, halo_recv, send_sem, recv_sem):
    me = lax.axis_index("blk")
    mine = lax.axis_index("comp")
    left, right = lax.rem(me + BLK - 1, BLK), lax.rem(me + 1, BLK)
    peers = offsets(me)
    friends = [lax.rem(mine + k, COMP) for k in range(1, COMP)]
    barrier = pltpu.get_barrier_semaphore()
    for p in peers:
        pl.semaphore_signal(barrier, inc=1, device_id={"blk": p}, device_id_type=MESH)
    for f in friends:
        pl.semaphore_signal(barrier, inc=1, device_id={"comp": f}, device_id_type=MESH)

    step = NB // CHUNKS
    loads = []
    for k in range(CHUNKS):
        b, r = pl.ds(k * step, step), pl.ds(k * step * 128, step * 128)
        trio = [pltpu.make_async_copy(e_hbm.at[b], e.at[b], load_sem.at[3 * k]),
                pltpu.make_async_copy(d_hbm.at[b], d.at[b], load_sem.at[3 * k + 1]),
                pltpu.make_async_copy(x_hbm.at[r], x.at[r], load_sem.at[3 * k + 2])]
        for t in trio:
            t.start()
        loads.append(trio)
    late = [pltpu.make_async_copy(m_hbm, m, load_sem.at[3 * CHUNKS]),
            pltpu.make_async_copy(c_hbm, cpl, load_sem.at[3 * CHUNKS + 1])]
    for t in late:
        t.start()

    has_left, has_right = me > 0, me < BLK - 1

    def put_a(b, col, block):
        hi, lo = split(block)
        ah[b, :, col * 128:(col + 1) * 128] = hi
        al[b, :, col * 128:(col + 1) * 128] = lo

    def build(b):
        link = e[b]
        put_a(b, 0, jnp.where(jnp.logical_or(has_left, b > 0), link, 0.0))
        put_a(b, 1, d[b])
        hi, lo = split(x[rows_at(b * 128, 128), :])
        xh[rows_at(b * 128 + 128, 128), :] = hi
        xl[rows_at(b * 128 + 128, 128), :] = lo
        put_a(jnp.where(b > 0, b - 1, NB - 1), 2, link.T)

    for k in range(CHUNKS):
        for t in loads[k]:
            t.wait()

        def builds(i, _, k=k):
            build(k * step + 2 * i)
            build(k * step + 2 * i + 1)
            return 0

        lax.fori_loop(0, step // 2, builds, 0)

    pl.semaphore_wait(barrier, len(peers) + len(friends))

    def send(src, dst, slot, peer):
        copy = pltpu.make_async_remote_copy(
            src_ref=src, dst_ref=dst, send_sem=halo_send.at[slot], recv_sem=halo_recv.at[slot],
            device_id={"blk": peer}, device_id_type=MESH)
        copy.start()
        return copy

    def copy(src, dst, phase, peer, slot, axis="blk"):
        return pltpu.make_async_remote_copy(
            src_ref=src, dst_ref=dst, send_sem=send_sem.at[phase, peer],
            recv_sem=recv_sem.at[phase, slot], device_id={axis: peer}, device_id_type=MESH)

    halos = [
        send(e.at[0], enext, 6, left),
        send(x.at[pl.ds(ROWS - 128, 128)], halo.at[0], 0, right),
        send(x.at[pl.ds(0, 128)], halo.at[1], 1, left),
    ]

    def product(vh, vl, p):
        out = []
        for q in range(2):
            s = rows_at(p * 256 + q * 128, 384)
            h, l, a = vh[s, :], vl[s, :], ah[2 * p + q]
            out.append(mm(cat([a, a, al[2 * p + q]], 1), cat([h, l, h], 0)))
        return cat(out, 0)

    def own(p):
        return rows_at(p * 256 + 128, 256)

    def apply_f(p):
        f = x[rows_at(p * 256, 256), :] * (1.0 / 256) - product(xh, xl, p) * (STEP / 256)
        fh[own(p), :], fl[own(p), :] = split(f)
        return f

    def apply_y(p):
        f = fh[own(p), :].astype(F32) + fl[own(p), :].astype(F32)
        y = f - product(fh, fl, p) * STEP
        yh[own(p), :], yl[own(p), :] = split(y)
        return y

    def apply_z(p):
        zh, zl = split(product(yh, yl, p))
        s = rows_at(p * 256, 256)
        th, tl = xh[s, :], xl[s, :]
        gram[1] = gram[1] + mm(cat([th, th, tl], 1), cat([zh, zl, zh], 0))

    def wait_halo(rnd, vh, vl):
        if rnd == 0:
            halos[0].wait()
            put_a(NB - 1, 2, jnp.where(has_right, enext[...], 0.0).T)
        halos[2 * rnd + 1].wait()
        vh[0:128, :], vl[0:128, :] = split(jnp.where(has_left, halo[2 * rnd], 0.0))
        halos[2 * rnd + 2].wait()
        vh[ROWS + 128:ROWS + 256, :], vl[ROWS + 128:ROWS + 256, :] = split(
            jnp.where(has_right, halo[2 * rnd + 1], 0.0))

    def pairs(fn, start, stop):
        def body(i, _):
            fn(start + 2 * i)
            fn(start + 2 * i + 1)
            return 0

        lax.fori_loop(0, (stop - start) // 2, body, 0)

    last_pair = NB // 2 - 1
    for rnd, (fn, vh, vl) in enumerate(((apply_f, xh, xl), (apply_y, fh, fl))):
        pairs(fn, 1, last_pair)
        wait_halo(rnd, vh, vl)
        edge[2 * rnd] = fn(last_pair)[128:, :]
        halos.append(send(edge.at[2 * rnd], halo.at[2 * rnd + 2], 2 * rnd + 2, right))
        edge[2 * rnd + 1] = fn(0)[:128, :]
        halos.append(send(edge.at[2 * rnd + 1], halo.at[2 * rnd + 3], 2 * rnd + 3, left))

    for t in late:
        t.wait()
    gram[...] = jnp.zeros_like(gram)
    cum[0] = jnp.zeros((256, 128), F32)

    def mass(p):
        h, l = yh[own(p), :], yl[own(p), :]
        parts = []
        for q in range(2):
            mh, ml = split(m[2 * p + q])
            s = slice(q * 128, (q + 1) * 128)
            both = mm(cat([cat([mh, mh], 1), cat([ml, ml], 1)], 0), cat([h[s], l[s]], 0))
            parts.append(both[:128] + both[128:])
        mh, ml = split(cat(parts, 0))
        th, tl = h.T, l.T
        xh[rows_at(p * 256, 256), :] = th
        xl[rows_at(p * 256, 256), :] = tl
        gram[0] = gram[0] + mm(cat([th, th, tl], 1), cat([mh, ml, mh], 0))
        for q in range(2):
            b = 2 * p + q
            ch, cl = split(cpl[b])
            cc = cat([ch, cl], 1)
            s = slice(q * 128, (q + 1) * 128)
            both = mm(cat([th[:, s], tl[:, s]], 1), cat([cc, cc], 0))
            cum[b + 1] = both[:, :128] + both[:, 128:] + cum[links[b]]

    pairs(mass, 0, NB // 2)

    def part(p):
        return rows_at(p * 16, 16)

    def reduce_out(t):
        out = [copy(gram.at[t, part(p)], gram_in.at[t, me], t, p, me) for p in peers]
        for c in out:
            c.start()
        return out

    def reduce_in(t):
        acc = gram[t, part(me), :]
        for p in peers:
            copy(gram.at[t, part(p)], gram_in.at[t, p], t, p, p).wait_recv()
            acc = acc + gram_in[t, p]
        sums[t, part(me), :] = acc
        piece = sums.at[t, part(me)]
        out = [copy(piece, piece, 2 + t, p, me) for p in peers]
        for c in out:
            c.start()
        return out

    def gathered(t):
        for p in peers:
            copy(sums.at[t, part(me)], sums.at[t, part(p)], 2 + t, p, p).wait_recv()

    started = reduce_out(0)

    def projection(j, _):
        w[j] = cum[links[NB + j]]
        return 0

    lax.fori_loop(0, BLK, projection, 0)
    w_out = [copy(w.at[p], w_in.at[me], 4, p, me) for p in peers]
    for c in w_out[:EARLY]:
        c.start()

    pairs(apply_z, 1, 9)
    started += reduce_in(0)
    pairs(apply_z, 9, last_pair)
    wait_halo(2, yh, yl)
    apply_z(0)
    apply_z(last_pair)
    started += reduce_out(1)
    started += reduce_in(1)
    for c in w_out[EARLY:]:
        c.start()
    gathered(0)
    gathered(1)

    size = 256
    row = lax.broadcasted_iota(jnp.int32, (size, size), 0)
    column = lax.broadcasted_iota(jnp.int32, (size, size), 1)
    for t in range(2):
        g = sums[t]
        fa[t] = (g + g.T) * 0.5
        fx[t] = jnp.where(row == column, 1.0, 0.0)
    for k in range(4):
        lo, hi = 64 * k, 64 * (k + 1)
        inv = diag_inverse([fa[t, lo:hi, lo:hi] for t in range(2)])
        for t in range(2):
            tri = inv[t][:, 64:]
            xu = mmh(tri, fx[t, lo:hi, :])
            fx[t, lo:hi, :] = xu
            if k < 3:
                au = mmh(tri, fa[t, lo:hi, :])
                low = au[:, hi:].T
                fa[t, hi:, :] = fa[t, hi:, :] - mmh(low, au)
                fx[t, hi:, :] = fx[t, hi:, :] - mmh(low, xu)

    total = w[me]
    for p in peers:
        copy(w.at[p], w_in.at[p], 4, p, p).wait_recv()
        total = total + w_in[p]
    scaled = mmh(fx[1], total)
    cond[...] = mmh(scaled.T, scaled)

    def eight(p):
        return rows_at(p * 8, 8)

    cond_out = [copy(cond.at[eight(p)], cond_in.at[me], 5, p, me) for p in peers]
    for c in cond_out:
        c.start()

    def modes(p):
        h, l = yh[own(p), :], yl[own(p), :]
        modes_ref[rows_at(p * 256, 256), :] = mm(cat([h, h, l], 1), ct[...])

    inverse = fx[0]
    turned = inverse.T
    red_ref[...] = mmh(mmh(inverse, sums[1]), turned)
    h, l = split(turned * 256.0)
    ct[...] = cat([h, l, h], 0)
    pairs(modes, 0, 4)
    cond_in[me] = cond[eight(me), :]
    for p in peers:
        copy(cond.at[eight(p)], cond_in.at[p], 5, p, p).wait_recv()
    pieces = [cond_in[i] for i in range(BLK)]
    for g in range(4 * COMP):
        dense[g] = sum(hot[g, i] * pieces[i] for i in range(BLK))

    def four(o):
        return pl.ds(o * 4, 4)

    dense_out = [copy(dense.at[four(f)], dense_in.at[mine], 6, f, mine, "comp") for f in friends]
    for c in dense_out:
        c.start()
    pairs(modes, 4, 10)
    acc = dense[four(mine)]
    for f in friends:
        copy(dense.at[four(f)], dense_in.at[f], 6, f, f, "comp").wait_recv()
        acc = acc + dense_in[f]
    slab[...] = acc
    slab_out = [copy(slab, slab_in.at[me], 7, p, me) for p in peers]
    for c in slab_out:
        c.start()
    asm_ref[:, eight(me), :] = acc
    pairs(modes, 10, 16)
    for p in peers:
        copy(slab, slab_in.at[p], 7, p, p).wait_recv()
        asm_ref[:, eight(p), :] = slab_in[p]
    for c in started + w_out + cond_out + dense_out + slab_out:
        c.wait_send()


def local(start_modes, stiff_diag, stiff_off, mass_blocks, coupling, interface_block, global_iface):
    ids = interface_block[0]
    order = jnp.arange(NB, dtype=jnp.int32)
    earlier = (ids[:, None] == ids[None, :]) & (order[None, :] < order[:, None])
    ends = jnp.arange(BLK, dtype=jnp.int32)[:, None] == ids[None, :]
    links = jnp.max(jnp.where(jnp.concatenate([earlier, ends], 0), order[None, :] + 1, 0), axis=1)
    hot = (jnp.arange(4 * COMP, dtype=jnp.int32)[:, None] == global_iface[0][None, :]).astype(F32)
    smem = pl.BlockSpec(memory_space=pltpu.SMEM)
    anym = pl.BlockSpec(memory_space=pl.ANY)
    vm = pl.BlockSpec(memory_space=pltpu.VMEM)
    ext = pltpu.VMEM((ROWS + 256, 256), BF)
    blocks = pltpu.VMEM((NB, 128, 128), F32)
    modes, reduced, assembled = pl.pallas_call(
        kernel,
        out_shape=(jax.ShapeDtypeStruct((ROWS, 256), F32),
                   jax.ShapeDtypeStruct((256, 256), F32),
                   jax.ShapeDtypeStruct((4, 128, 128), F32)),
        in_specs=[smem, smem] + [anym] * 5,
        out_specs=(vm,) * 3,
        scratch_shapes=[
            pltpu.VMEM((ROWS, 256), F32), blocks, blocks, blocks, blocks,
            ext, ext, ext, ext, ext, ext,
            pltpu.VMEM((NB, 128, 384), BF), pltpu.VMEM((NB, 128, 384), BF),
            pltpu.VMEM((NB + 1, 256, 128), F32),
            pltpu.VMEM((768, 256), BF),
            pltpu.VMEM((4, 128, 256), F32),
            pltpu.VMEM((6, 128, 256), F32),
            pltpu.VMEM((128, 128), F32),
            pltpu.VMEM((2, 256, 256), F32),
            pltpu.VMEM((2, BLK, 16, 256), F32),
            pltpu.VMEM((2, 256, 256), F32),
            pltpu.VMEM((BLK, 256, 128), F32),
            pltpu.VMEM((BLK, 256, 128), F32),
            pltpu.VMEM((2, 256, 256), F32),
            pltpu.VMEM((2, 256, 256), F32),
            pltpu.VMEM((128, 128), F32),
            pltpu.VMEM((BLK, 8, 128), F32),
            pltpu.VMEM((4 * COMP, 8, 128), F32),
            pltpu.VMEM((COMP, 4, 8, 128), F32),
            pltpu.VMEM((4, 8, 128), F32),
            pltpu.VMEM((BLK, 4, 8, 128), F32),
            pltpu.SemaphoreType.DMA((3 * CHUNKS + 2,)),
            pltpu.SemaphoreType.DMA((7,)),
            pltpu.SemaphoreType.DMA((7,)),
            pltpu.SemaphoreType.DMA((8, 16)),
            pltpu.SemaphoreType.DMA((8, 16)),
        ],
        compiler_params=pltpu.CompilerParams(
            collective_id=0, has_side_effects=True, vmem_limit_bytes=60 * MIB),
        name="superelement",
    )(links, hot, start_modes[0], stiff_diag[0], stiff_off[0], mass_blocks[0], coupling[0])
    return modes[None], reduced[None], assembled


def solution(mesh):
    in_specs = (
        P("comp", "blk", None),
        P("comp", "blk", None, None),
        P("comp", "blk", None, None),
        P("comp", "blk", None, None),
        P("comp", "blk", None, None),
        P("comp", "blk"),
        P("comp", None),
    )
    out_specs = (P("comp", "blk", None), P("comp", None, None), P("comp", None, None))
    return jax.shard_map(local, mesh=mesh, in_specs=in_specs, out_specs=out_specs, check_vma=False)
```

```python
import functools

import jax
import jax.numpy as jnp
from jax import lax
from jax.experimental import pallas as pl
from jax.experimental.pallas import tpu as pltpu
from jax.sharding import PartitionSpec as P

BF = jnp.bfloat16
F32 = jnp.float32
STEP = 0.15
MESH = pl.DeviceIdType.MESH
HI = lax.Precision.HIGHEST
MIB = 1 << 20
NB = 32
ROWS = NB * 128
BLK = 16
COMP = 8
CHUNKS = 4
EARLY = 6


def split(x):
    hi = x.astype(BF)
    lo = (x - hi.astype(F32)).astype(BF)
    return hi, lo


def mm(a, b):
    return jnp.dot(a, b, preferred_element_type=F32)


def mmh(a, b):
    return jnp.dot(a, b, preferred_element_type=F32, precision=HI)


def cat(parts, axis):
    return jnp.concatenate(parts, axis)


def rows_at(start, size):
    return pl.ds(pl.multiple_of(start, min(size, 128)), size)


def diag_inverse(mats):
    groups = 8
    sub = lax.broadcasted_iota(jnp.int32, (8, 128), 0)
    lane = lax.broadcasted_iota(jnp.int32, (8, 128), 1)
    state = []
    for mat in mats:
        full = cat([mat, jnp.zeros_like(mat)], 1)
        state.append([
            jnp.where(lane == sub + (64 + 8 * g), 1.0, full[8 * g:8 * g + 8]) for g in range(groups)
        ])
    for k in range(groups):
        cols = [[[jnp.broadcast_to(rows[g][:, 8 * k + c:8 * k + c + 1], (8, 128)) for c in range(8)]
                 for g in range(k, groups)] for rows in state]
        for c in range(8):
            for rows, col in zip(state, cols):
                mine = col[0]
                rs = lax.rsqrt(jnp.broadcast_to(mine[c][c:c + 1, :], (8, 128)))
                u = jnp.broadcast_to(rows[k][c:c + 1, :], (8, 128)) * rs
                heads = {n: jnp.broadcast_to(mine[n][c:c + 1, :], (8, 128)) * rs for n in range(c + 1, 8)}
                for g in range(k, groups):
                    mult = col[g - k][c] * rs
                    if g == k:
                        mult = jnp.where(sub > c, mult, 0.0)
                        rows[g] = jnp.where(sub == c, u, rows[g] - mult * u)
                    else:
                        rows[g] = rows[g] - mult * u
                    for n in range(c + 1, 8):
                        col[g - k][n] = col[g - k][n] - mult * heads[n]
    return [cat(rows, 0) for rows in state]


def offsets(me):
    y, z = me // 4, lax.rem(me, 4)
    turns = ((0, 1), (1, 0), (0, 3), (3, 0), (1, 1), (3, 3), (1, 3), (3, 1),
             (0, 2), (2, 0), (1, 2), (2, 1), (3, 2), (2, 3), (2, 2))
    return [lax.rem(y + dy, 4) * 4 + lax.rem(z + dz, 4) for dy, dz in turns]


def kernel(ids, owned, x_hbm, d_hbm, e_hbm, m_hbm, c_hbm, yh, yl, ct, red_ref, asm_ref,
           x, d, e, m, cpl, xh, xl, fh, fl, ah, al, cum,
           edge, halo, enext, gram, gram_in, sums, w, w_in, fa, fx,
           cond, cond_in, dense, dense_in, slab, slab_in,
           load_sem, halo_send, halo_recv, send_sem, recv_sem):
    me = lax.axis_index("blk")
    mine = lax.axis_index("comp")
    left, right = lax.rem(me + BLK - 1, BLK), lax.rem(me + 1, BLK)
    peers = offsets(me)
    friends = [lax.rem(mine + k, COMP) for k in range(1, COMP)]
    barrier = pltpu.get_barrier_semaphore()
    for p in peers:
        pl.semaphore_signal(barrier, inc=1, device_id={"blk": p}, device_id_type=MESH)
    for f in friends:
        pl.semaphore_signal(barrier, inc=1, device_id={"comp": f}, device_id_type=MESH)

    step = NB // CHUNKS
    loads = []
    for k in range(CHUNKS):
        b, r = pl.ds(k * step, step), pl.ds(k * step * 128, step * 128)
        trio = [pltpu.make_async_copy(e_hbm.at[b], e.at[b], load_sem.at[3 * k]),
                pltpu.make_async_copy(d_hbm.at[b], d.at[b], load_sem.at[3 * k + 1]),
                pltpu.make_async_copy(x_hbm.at[r], x.at[r], load_sem.at[3 * k + 2])]
        for t in trio:
            t.start()
        loads.append(trio)
    late = [pltpu.make_async_copy(m_hbm, m, load_sem.at[3 * CHUNKS]),
            pltpu.make_async_copy(c_hbm, cpl, load_sem.at[3 * CHUNKS + 1])]
    for t in late:
        t.start()

    has_left, has_right = me > 0, me < BLK - 1

    def put_a(b, col, block):
        hi, lo = split(block)
        ah[b, :, col * 128:(col + 1) * 128] = hi
        al[b, :, col * 128:(col + 1) * 128] = lo

    def build(b):
        link = e[b]
        put_a(b, 0, jnp.where(jnp.logical_or(has_left, b > 0), link, 0.0))
        put_a(b, 1, d[b])
        hi, lo = split(x[rows_at(b * 128, 128), :])
        xh[rows_at(b * 128 + 128, 128), :] = hi
        xl[rows_at(b * 128 + 128, 128), :] = lo
        put_a(jnp.where(b > 0, b - 1, NB - 1), 2, link.T)

    def send(src, dst, slot, peer):
        copy = pltpu.make_async_remote_copy(
            src_ref=src, dst_ref=dst, send_sem=halo_send.at[slot], recv_sem=halo_recv.at[slot],
            device_id={"blk": peer}, device_id_type=MESH)
        copy.start()
        return copy

    def copy(src, dst, phase, peer, slot, axis="blk"):
        return pltpu.make_async_remote_copy(
            src_ref=src, dst_ref=dst, send_sem=send_sem.at[phase, peer],
            recv_sem=recv_sem.at[phase, slot], device_id={axis: peer}, device_id_type=MESH)

    def product(vh, vl, p):
        out = []
        for q in range(2):
            s = rows_at(p * 256 + q * 128, 384)
            h, l, a = vh[s, :], vl[s, :], ah[2 * p + q]
            out.append(mm(cat([a, a, al[2 * p + q]], 1), cat([h, l, h], 0)))
        return cat(out, 0)

    def own(p):
        return rows_at(p * 256 + 128, 256)

    def apply_f(p):
        f = x[rows_at(p * 256, 256), :] * (1.0 / 256) - product(xh, xl, p) * (STEP / 256)
        fh[own(p), :], fl[own(p), :] = split(f)
        return f

    def apply_y(p):
        f = fh[own(p), :].astype(F32) + fl[own(p), :].astype(F32)
        y = f - product(fh, fl, p) * STEP
        yh[own(p), :], yl[own(p), :] = split(y)
        return y

    def apply_z(p):
        zh, zl = split(product(yh, yl, p))
        s = rows_at(p * 256, 256)
        th, tl = xh[s, :], xl[s, :]
        gram[1] = gram[1] + mm(cat([th, th, tl], 1), cat([zh, zl, zh], 0))

    def wait_halo(rnd, vh, vl):
        if rnd == 0:
            halos[0].wait()
            put_a(NB - 1, 2, jnp.where(has_right, enext[...], 0.0).T)
        halos[2 * rnd + 1].wait()
        vh[0:128, :], vl[0:128, :] = split(jnp.where(has_left, halo[2 * rnd], 0.0))
        halos[2 * rnd + 2].wait()
        vh[ROWS + 128:ROWS + 256, :], vl[ROWS + 128:ROWS + 256, :] = split(
            jnp.where(has_right, halo[2 * rnd + 1], 0.0))

    def pairs(fn, start, stop):
        def body(i, _):
            fn(start + 2 * i)
            fn(start + 2 * i + 1)
            return 0

        lax.fori_loop(0, (stop - start) // 2, body, 0)

    last_pair = NB // 2 - 1
    for k in range(CHUNKS):
        for t in loads[k]:
            t.wait()
        if k == 2:
            pl.semaphore_wait(barrier, len(peers) + len(friends))
            halos = [
                send(e_hbm.at[0], enext, 6, left),
                send(x_hbm.at[pl.ds(ROWS - 128, 128)], halo.at[0], 0, right),
                send(x_hbm.at[pl.ds(0, 128)], halo.at[1], 1, left),
            ]
        first = k * step // 2
        if k == 0:
            for p in range(3):
                build(2 * p)
                build(2 * p + 1)
            apply_f(1)
            build(6)
            build(7)
        else:
            def both(i, _, first=first):
                for u in range(2):
                    p = first + 2 * i + u
                    apply_f(p - 2)
                    build(2 * p)
                    build(2 * p + 1)
                return 0

            lax.fori_loop(0, step // 4, both, 0)
    apply_f(last_pair - 1)

    for rnd, (fn, vh, vl) in enumerate(((apply_f, xh, xl), (apply_y, fh, fl))):
        if rnd:
            pairs(fn, 1, last_pair)
        wait_halo(rnd, vh, vl)
        edge[2 * rnd] = fn(last_pair)[128:, :]
        halos.append(send(edge.at[2 * rnd], halo.at[2 * rnd + 2], 2 * rnd + 2, right))
        edge[2 * rnd + 1] = fn(0)[:128, :]
        halos.append(send(edge.at[2 * rnd + 1], halo.at[2 * rnd + 3], 2 * rnd + 3, left))

    for t in late:
        t.wait()
    gram[...] = jnp.zeros_like(gram)
    cum[0] = jnp.zeros((256, 128), F32)

    def before(b):
        slot = 0
        for q in range(NB):
            slot = jnp.where(jnp.logical_and(ids[q] == ids[b], q < b), q + 1, slot)
        return slot

    def final(j):
        slot = 0
        for q in range(NB):
            slot = jnp.where(ids[q] == j, q + 1, slot)
        return slot

    def mass(p):
        h, l = yh[own(p), :], yl[own(p), :]
        parts = []
        for q in range(2):
            mh, ml = split(m[2 * p + q])
            s = slice(q * 128, (q + 1) * 128)
            both = mm(cat([cat([mh, mh], 1), cat([ml, ml], 1)], 0), cat([h[s], l[s]], 0))
            parts.append(both[:128] + both[128:])
        mh, ml = split(cat(parts, 0))
        th, tl = h.T, l.T
        xh[rows_at(p * 256, 256), :] = th
        xl[rows_at(p * 256, 256), :] = tl
        gram[0] = gram[0] + mm(cat([th, th, tl], 1), cat([mh, ml, mh], 0))
        for q in range(2):
            b = 2 * p + q
            ch, cl = split(cpl[b])
            cc = cat([ch, cl], 1)
            s = slice(q * 128, (q + 1) * 128)
            both = mm(cat([th[:, s], tl[:, s]], 1), cat([cc, cc], 0))
            cum[b + 1] = both[:, :128] + both[:, 128:] + cum[before(b)]

    pairs(mass, 0, NB // 2)

    def part(p):
        return rows_at(p * 16, 16)

    def reduce_out(t):
        out = [copy(gram.at[t, part(p)], gram_in.at[t, me], t, p, me) for p in peers]
        for c in out:
            c.start()
        return out

    def reduce_in(t):
        acc = gram[t, part(me), :]
        for p in peers:
            copy(gram.at[t, part(p)], gram_in.at[t, p], t, p, p).wait_recv()
            acc = acc + gram_in[t, p]
        sums[t, part(me), :] = acc
        piece = sums.at[t, part(me)]
        out = [copy(piece, piece, 2 + t, p, me) for p in peers]
        for c in out:
            c.start()
        return out

    def gathered(t):
        for p in peers:
            copy(sums.at[t, part(me)], sums.at[t, part(p)], 2 + t, p, p).wait_recv()

    started = reduce_out(0)

    def projection(j, _):
        w[j] = cum[final(j)]
        return 0

    lax.fori_loop(0, BLK, projection, 0)
    w_out = [copy(w.at[p], w_in.at[me], 4, p, me) for p in peers]
    for c in w_out[:EARLY]:
        c.start()

    pairs(apply_z, 1, last_pair)
    started += reduce_in(0)
    wait_halo(2, yh, yl)
    apply_z(0)
    apply_z(last_pair)
    started += reduce_out(1)
    started += reduce_in(1)
    for c in w_out[EARLY:]:
        c.start()
    gathered(0)
    gathered(1)

    size = 256
    row = lax.broadcasted_iota(jnp.int32, (size, size), 0)
    column = lax.broadcasted_iota(jnp.int32, (size, size), 1)
    for t in range(2):
        g = sums[t]
        fa[t] = (g + g.T) * 0.5
        fx[t] = jnp.where(row == column, 1.0, 0.0)
    for k in range(4):
        lo, hi = 64 * k, 64 * (k + 1)
        inv = diag_inverse([fa[t, lo:hi, lo:hi] for t in range(2)])
        for t in range(2):
            tri = inv[t][:, 64:]
            xu = mmh(tri, fx[t, lo:hi, :])
            fx[t, lo:hi, :] = xu
            if k < 3:
                au = mmh(tri, fa[t, lo:hi, :])
                low = au[:, hi:].T
                fa[t, hi:, :] = fa[t, hi:, :] - mmh(low, au)
                fx[t, hi:, :] = fx[t, hi:, :] - mmh(low, xu)

    total = w[me]
    for p in peers:
        copy(w.at[p], w_in.at[p], 4, p, p).wait_recv()
        total = total + w_in[p]
    scaled = mmh(fx[1], total)
    cond[...] = mmh(scaled.T, scaled)

    def eight(p):
        return rows_at(p * 8, 8)

    cond_out = [copy(cond.at[eight(p)], cond_in.at[me], 5, p, me) for p in peers]
    for c in cond_out:
        c.start()

    inverse = fx[0]
    turned = inverse.T
    red_ref[...] = mmh(mmh(inverse, sums[1]), turned)
    h, l = split(turned * 256.0)
    ct[...] = cat([h, l, h], 0)
    cond_in[me] = cond[eight(me), :]
    for p in peers:
        copy(cond.at[eight(p)], cond_in.at[p], 5, p, p).wait_recv()
    pieces = [cond_in[i] for i in range(BLK)]
    for g in range(4 * COMP):
        dense[g] = sum(jnp.where(owned[i] == g, 1.0, 0.0) * pieces[i] for i in range(BLK))

    def four(o):
        return pl.ds(o * 4, 4)

    dense_out = [copy(dense.at[four(f)], dense_in.at[mine], 6, f, mine, "comp") for f in friends]
    for c in dense_out:
        c.start()
    acc = dense[four(mine)]
    for f in friends:
        copy(dense.at[four(f)], dense_in.at[f], 6, f, f, "comp").wait_recv()
        acc = acc + dense_in[f]
    slab[...] = acc
    slab_out = [copy(slab, slab_in.at[me], 7, p, me) for p in peers]
    for c in slab_out:
        c.start()
    asm_ref[:, eight(me), :] = acc
    for p in peers:
        copy(slab, slab_in.at[p], 7, p, p).wait_recv()
        asm_ref[:, eight(p), :] = slab_in[p]
    for c in started + w_out + cond_out + dense_out + slab_out:
        c.wait_send()


def result_kernel(yh, yl, ct, red, asm, modes_ref, red_ref, asm_ref, sem):
    i = pl.program_id(0)
    tile = modes_ref.shape[0]
    moves = [pltpu.make_async_copy(red, red_ref, sem.at[0]), pltpu.make_async_copy(asm, asm_ref, sem.at[1])]

    @pl.when(i == 0)
    def _():
        for t in moves:
            t.start()

    for q in range(tile // 256):
        s = rows_at(i * tile + q * 256 + 128, 256)
        h = yh[s, :]
        modes_ref[q * 256:(q + 1) * 256, :] = mm(cat([h, h, yl[s, :]], 1), ct[...])

    @pl.when(i == pl.num_programs(0) - 1)
    def _():
        for t in moves:
            t.wait()


def local(start_modes, stiff_diag, stiff_off, mass_blocks, coupling, interface_block, global_iface):
    smem = pl.BlockSpec(memory_space=pltpu.SMEM)
    hbm = pl.BlockSpec(memory_space=pltpu.HBM)
    anym = pl.BlockSpec(memory_space=pl.ANY)
    vm = pl.BlockSpec(memory_space=pltpu.VMEM)
    ext = pltpu.VMEM((ROWS + 256, 256), BF)
    blocks = pltpu.VMEM((NB, 128, 128), F32)
    yh, yl, ct, reduced, assembled = pl.pallas_call(
        kernel,
        out_shape=(ext, ext, pltpu.VMEM((768, 256), BF), pltpu.VMEM((256, 256), F32),
                   pltpu.VMEM((4, 128, 128), F32)),
        in_specs=[smem, smem] + [hbm] * 5,
        out_specs=(vm,) * 5,
        scratch_shapes=[
            pltpu.VMEM((ROWS, 256), F32), blocks, blocks, blocks, blocks,
            ext, ext, ext, ext,
            pltpu.VMEM((NB, 128, 384), BF), pltpu.VMEM((NB, 128, 384), BF),
            pltpu.VMEM((NB + 1, 256, 128), F32),
            pltpu.VMEM((4, 128, 256), F32),
            pltpu.VMEM((6, 128, 256), F32),
            pltpu.VMEM((128, 128), F32),
            pltpu.VMEM((2, 256, 256), F32),
            pltpu.VMEM((2, BLK, 16, 256), F32),
            pltpu.VMEM((2, 256, 256), F32),
            pltpu.VMEM((BLK, 256, 128), F32),
            pltpu.VMEM((BLK, 256, 128), F32),
            pltpu.VMEM((2, 256, 256), F32),
            pltpu.VMEM((2, 256, 256), F32),
            pltpu.VMEM((128, 128), F32),
            pltpu.VMEM((BLK, 8, 128), F32),
            pltpu.VMEM((4 * COMP, 8, 128), F32),
            pltpu.VMEM((COMP, 4, 8, 128), F32),
            pltpu.VMEM((4, 8, 128), F32),
            pltpu.VMEM((BLK, 4, 8, 128), F32),
            pltpu.SemaphoreType.DMA((3 * CHUNKS + 2,)),
            pltpu.SemaphoreType.DMA((7,)),
            pltpu.SemaphoreType.DMA((7,)),
            pltpu.SemaphoreType.DMA((8, 16)),
            pltpu.SemaphoreType.DMA((8, 16)),
        ],
        compiler_params=pltpu.CompilerParams(
            collective_id=0, has_side_effects=True, vmem_limit_bytes=48 * MIB),
        name="superelement",
    )(interface_block[0], global_iface[0], start_modes[0], stiff_diag[0], stiff_off[0],
      mass_blocks[0], coupling[0])
    tile = 512
    modes, reduced, assembled = pl.pallas_call(
        result_kernel,
        out_shape=(jax.ShapeDtypeStruct((ROWS, 256), F32),
                   jax.ShapeDtypeStruct((256, 256), F32),
                   jax.ShapeDtypeStruct((4, 128, 128), F32)),
        grid=(ROWS // tile,),
        in_specs=[vm] * 5,
        out_specs=(pl.BlockSpec((tile, 256), lambda i: (i, 0)), anym, anym),
        scratch_shapes=[pltpu.SemaphoreType.DMA((2,))],
        compiler_params=pltpu.CompilerParams(vmem_limit_bytes=12 * MIB),
        name="result",
    )(yh, yl, ct, reduced, assembled)
    return modes[None], reduced[None], assembled


def solution(mesh):
    in_specs = (
        P("comp", "blk", None),
        P("comp", "blk", None, None),
        P("comp", "blk", None, None),
        P("comp", "blk", None, None),
        P("comp", "blk", None, None),
        P("comp", "blk"),
        P("comp", None),
    )
    out_specs = (P("comp", "blk", None), P("comp", None, None), P("comp", None, None))
    return jax.shard_map(local, mesh=mesh, in_specs=in_specs, out_specs=out_specs, check_vma=False)
```

```python
import functools

import jax
import jax.numpy as jnp
from jax import lax
from jax.experimental import pallas as pl
from jax.experimental.pallas import tpu as pltpu
from jax.sharding import PartitionSpec as P

BF = jnp.bfloat16
F32 = jnp.float32
STEP = 0.15
MESH = pl.DeviceIdType.MESH
HI = lax.Precision.HIGHEST
MIB = 1 << 20
NB = 32
ROWS = NB * 128
BLK = 16
COMP = 8
CHUNKS = 4
PARTS = 8
EARLY = 6


def split(x):
    hi = x.astype(BF)
    lo = (x - hi.astype(F32)).astype(BF)
    return hi, lo


def mm(a, b):
    return jnp.dot(a, b, preferred_element_type=F32)


def mmh(a, b):
    return jnp.dot(a, b, preferred_element_type=F32, precision=HI)


def cat(parts, axis):
    return jnp.concatenate(parts, axis)


def rows_at(start, size):
    return pl.ds(pl.multiple_of(start, min(size, 128)), size)


def diag_inverse(mats):
    groups = 8
    sub = lax.broadcasted_iota(jnp.int32, (8, 128), 0)
    lane = lax.broadcasted_iota(jnp.int32, (8, 128), 1)
    state = []
    for mat in mats:
        full = cat([mat, jnp.zeros_like(mat)], 1)
        state.append([
            jnp.where(lane == sub + (64 + 8 * g), 1.0, full[8 * g:8 * g + 8]) for g in range(groups)
        ])
    for k in range(groups):
        cols = [[[jnp.broadcast_to(rows[g][:, 8 * k + c:8 * k + c + 1], (8, 128)) for c in range(8)]
                 for g in range(k, groups)] for rows in state]
        for c in range(8):
            for rows, col in zip(state, cols):
                mine = col[0]
                rs = lax.rsqrt(jnp.broadcast_to(mine[c][c:c + 1, :], (8, 128)))
                u = jnp.broadcast_to(rows[k][c:c + 1, :], (8, 128)) * rs
                heads = {n: jnp.broadcast_to(mine[n][c:c + 1, :], (8, 128)) * rs for n in range(c + 1, 8)}
                for g in range(k, groups):
                    mult = col[g - k][c] * rs
                    if g == k:
                        mult = jnp.where(sub > c, mult, 0.0)
                        rows[g] = jnp.where(sub == c, u, rows[g] - mult * u)
                    else:
                        rows[g] = rows[g] - mult * u
                    for n in range(c + 1, 8):
                        col[g - k][n] = col[g - k][n] - mult * heads[n]
    return [cat(rows, 0) for rows in state]


def offsets(me):
    y, z = me // 4, lax.rem(me, 4)
    turns = ((0, 1), (1, 0), (0, 3), (3, 0), (1, 1), (3, 3), (1, 3), (3, 1),
             (0, 2), (2, 0), (1, 2), (2, 1), (3, 2), (2, 3), (2, 2))
    return [lax.rem(y + dy, 4) * 4 + lax.rem(z + dz, 4) for dy, dz in turns]


def kernel(ids_hbm, owned_hbm, x_hbm, d_hbm, e_hbm, m_hbm, c_hbm, modes_ref, red_ref, asm_ref,
           ids, owned, x, d, e, m, cpl, xh, xl, fh, fl, yh, yl, ah, al, cum, ct,
           edge, halo, enext, gram, gram_in, sums, w, w_in, fa, fx,
           cond, cond_in, dense, dense_in, slab, slab_in,
           load_sem, halo_send, halo_recv, send_sem, recv_sem):
    me = lax.axis_index("blk")
    mine = lax.axis_index("comp")
    left, right = lax.rem(me + BLK - 1, BLK), lax.rem(me + 1, BLK)
    peers = offsets(me)
    friends = [lax.rem(mine + k, COMP) for k in range(1, COMP)]
    barrier = pltpu.get_barrier_semaphore()
    for p in peers:
        pl.semaphore_signal(barrier, inc=1, device_id={"blk": p}, device_id_type=MESH)
    for f in friends:
        pl.semaphore_signal(barrier, inc=1, device_id={"comp": f}, device_id_type=MESH)

    step = NB // CHUNKS
    loads = []
    for k in range(CHUNKS):
        b, r = pl.ds(k * step, step), pl.ds(k * step * 128, step * 128)
        trio = [pltpu.make_async_copy(e_hbm.at[b], e.at[b], load_sem.at[3 * k]),
                pltpu.make_async_copy(d_hbm.at[b], d.at[b], load_sem.at[3 * k + 1]),
                pltpu.make_async_copy(x_hbm.at[r], x.at[r], load_sem.at[3 * k + 2])]
        for t in trio:
            t.start()
        loads.append(trio)
    late = [pltpu.make_async_copy(m_hbm, m, load_sem.at[3 * CHUNKS]),
            pltpu.make_async_copy(c_hbm, cpl, load_sem.at[3 * CHUNKS + 1]),
            pltpu.make_async_copy(ids_hbm, ids, load_sem.at[3 * CHUNKS + 2]),
            pltpu.make_async_copy(owned_hbm, owned, load_sem.at[3 * CHUNKS + 3])]

    has_left, has_right = me > 0, me < BLK - 1

    def put_a(b, col, block):
        hi, lo = split(block)
        ah[b, :, col * 128:(col + 1) * 128] = hi
        al[b, :, col * 128:(col + 1) * 128] = lo

    def build(b):
        link = e[b]
        put_a(b, 0, jnp.where(jnp.logical_or(has_left, b > 0), link, 0.0))
        put_a(b, 1, d[b])
        hi, lo = split(x[rows_at(b * 128, 128), :])
        xh[rows_at(b * 128 + 128, 128), :] = hi
        xl[rows_at(b * 128 + 128, 128), :] = lo
        put_a(jnp.where(b > 0, b - 1, NB - 1), 2, link.T)

    def send(src, dst, slot, peer):
        copy = pltpu.make_async_remote_copy(
            src_ref=src, dst_ref=dst, send_sem=halo_send.at[slot], recv_sem=halo_recv.at[slot],
            device_id={"blk": peer}, device_id_type=MESH)
        copy.start()
        return copy

    def copy(src, dst, phase, peer, slot, axis="blk"):
        return pltpu.make_async_remote_copy(
            src_ref=src, dst_ref=dst, send_sem=send_sem.at[phase, peer],
            recv_sem=recv_sem.at[phase, slot], device_id={axis: peer}, device_id_type=MESH)

    def product(vh, vl, p):
        out = []
        for q in range(2):
            s = rows_at(p * 256 + q * 128, 384)
            h, l, a = vh[s, :], vl[s, :], ah[2 * p + q]
            out.append(mm(cat([a, a, al[2 * p + q]], 1), cat([h, l, h], 0)))
        return cat(out, 0)

    def own(p):
        return rows_at(p * 256 + 128, 256)

    def apply_f(p):
        f = x[rows_at(p * 256, 256), :] * (1.0 / 256) - product(xh, xl, p) * (STEP / 256)
        fh[own(p), :], fl[own(p), :] = split(f)
        return f

    def apply_y(p):
        f = fh[own(p), :].astype(F32) + fl[own(p), :].astype(F32)
        y = f - product(fh, fl, p) * STEP
        yh[own(p), :], yl[own(p), :] = split(y)
        return y

    def apply_z(p):
        zh, zl = split(product(yh, yl, p))
        s = rows_at(p * 256, 256)
        th, tl = xh[s, :], xl[s, :]
        gram[1] = gram[1] + mm(cat([th, th, tl], 1), cat([zh, zl, zh], 0))

    def wait_halo(rnd, vh, vl):
        if rnd == 0:
            halos[0].wait()
            put_a(NB - 1, 2, jnp.where(has_right, enext[...], 0.0).T)
        halos[2 * rnd + 1].wait()
        vh[0:128, :], vl[0:128, :] = split(jnp.where(has_left, halo[2 * rnd], 0.0))
        halos[2 * rnd + 2].wait()
        vh[ROWS + 128:ROWS + 256, :], vl[ROWS + 128:ROWS + 256, :] = split(
            jnp.where(has_right, halo[2 * rnd + 1], 0.0))

    def pairs(fn, start, stop):
        def body(i, _):
            fn(start + 2 * i)
            fn(start + 2 * i + 1)
            return 0

        lax.fori_loop(0, (stop - start) // 2, body, 0)

    last_pair = NB // 2 - 1
    for k in range(CHUNKS):
        for t in loads[k]:
            t.wait()
        if k == 2:
            for t in late:
                t.start()
            pl.semaphore_wait(barrier, len(peers) + len(friends))
            halos = [
                send(e_hbm.at[0], enext, 6, left),
                send(x_hbm.at[pl.ds(ROWS - 128, 128)], halo.at[0], 0, right),
                send(x_hbm.at[pl.ds(0, 128)], halo.at[1], 1, left),
            ]
        first = k * step // 2
        if k == 0:
            for p in range(3):
                build(2 * p)
                build(2 * p + 1)
            apply_f(1)
            build(6)
            build(7)
        else:
            def both(i, _, first=first):
                for u in range(2):
                    p = first + 2 * i + u
                    apply_f(p - 2)
                    build(2 * p)
                    build(2 * p + 1)
                return 0

            lax.fori_loop(0, step // 4, both, 0)
    apply_f(last_pair - 1)

    for rnd, (fn, vh, vl) in enumerate(((apply_f, xh, xl), (apply_y, fh, fl))):
        if rnd:
            pairs(fn, 1, last_pair)
        wait_halo(rnd, vh, vl)
        edge[2 * rnd] = fn(last_pair)[128:, :]
        halos.append(send(edge.at[2 * rnd], halo.at[2 * rnd + 2], 2 * rnd + 2, right))
        edge[2 * rnd + 1] = fn(0)[:128, :]
        halos.append(send(edge.at[2 * rnd + 1], halo.at[2 * rnd + 3], 2 * rnd + 3, left))

    for t in late:
        t.wait()
    gram[...] = jnp.zeros_like(gram)
    cum[0] = jnp.zeros((256, 128), F32)

    def before(b):
        slot = 0
        for q in range(NB):
            slot = jnp.where(jnp.logical_and(ids[q] == ids[b], q < b), q + 1, slot)
        return slot

    def final(j):
        slot = 0
        for q in range(NB):
            slot = jnp.where(ids[q] == j, q + 1, slot)
        return slot

    def mass(p):
        h, l = yh[own(p), :], yl[own(p), :]
        parts = []
        for q in range(2):
            mh, ml = split(m[2 * p + q])
            s = slice(q * 128, (q + 1) * 128)
            both = mm(cat([cat([mh, mh], 1), cat([ml, ml], 1)], 0), cat([h[s], l[s]], 0))
            parts.append(both[:128] + both[128:])
        mh, ml = split(cat(parts, 0))
        th, tl = h.T, l.T
        xh[rows_at(p * 256, 256), :] = th
        xl[rows_at(p * 256, 256), :] = tl
        gram[0] = gram[0] + mm(cat([th, th, tl], 1), cat([mh, ml, mh], 0))
        for q in range(2):
            b = 2 * p + q
            ch, cl = split(cpl[b])
            cc = cat([ch, cl], 1)
            s = slice(q * 128, (q + 1) * 128)
            both = mm(cat([th[:, s], tl[:, s]], 1), cat([cc, cc], 0))
            cum[b + 1] = both[:, :128] + both[:, 128:] + cum[before(b)]

    pairs(mass, 0, NB // 2)

    def part(p):
        return rows_at(p * 16, 16)

    def reduce_out(t):
        out = [copy(gram.at[t, part(p)], gram_in.at[t, me], t, p, me) for p in peers]
        for c in out:
            c.start()
        return out

    def reduce_in(t):
        acc = gram[t, part(me), :]
        for p in peers:
            copy(gram.at[t, part(p)], gram_in.at[t, p], t, p, p).wait_recv()
            acc = acc + gram_in[t, p]
        sums[t, part(me), :] = acc
        piece = sums.at[t, part(me)]
        out = [copy(piece, piece, 2 + t, p, me) for p in peers]
        for c in out:
            c.start()
        return out

    def gathered(t):
        for p in peers:
            copy(sums.at[t, part(me)], sums.at[t, part(p)], 2 + t, p, p).wait_recv()

    started = reduce_out(0)

    def projection(j, _):
        w[j] = cum[final(j)]
        return 0

    lax.fori_loop(0, BLK, projection, 0)
    w_out = [copy(w.at[p], w_in.at[me], 4, p, me) for p in peers]
    for c in w_out[:EARLY]:
        c.start()

    pairs(apply_z, 1, 11)
    started += reduce_in(0)
    pairs(apply_z, 11, last_pair)
    wait_halo(2, yh, yl)
    apply_z(0)
    apply_z(last_pair)
    started += reduce_out(1)
    started += reduce_in(1)
    for c in w_out[EARLY:]:
        c.start()
    gathered(0)
    gathered(1)

    size = 256
    row = lax.broadcasted_iota(jnp.int32, (size, size), 0)
    column = lax.broadcasted_iota(jnp.int32, (size, size), 1)
    for t in range(2):
        g = sums[t]
        fa[t] = (g + g.T) * 0.5
        fx[t] = jnp.where(row == column, 1.0, 0.0)
    for k in range(4):
        lo, hi = 64 * k, 64 * (k + 1)
        inv = diag_inverse([fa[t, lo:hi, lo:hi] for t in range(2)])
        for t in range(2):
            tri = inv[t][:, 64:]
            xu = mmh(tri, fx[t, lo:hi, :])
            fx[t, lo:hi, :] = xu
            if k < 3:
                au = mmh(tri, fa[t, lo:hi, :])
                low = au[:, hi:].T
                fa[t, hi:, :] = fa[t, hi:, :] - mmh(low, au)
                fx[t, hi:, :] = fx[t, hi:, :] - mmh(low, xu)

    total = w[me]
    for p in peers:
        copy(w.at[p], w_in.at[p], 4, p, p).wait_recv()
        total = total + w_in[p]
    scaled = mmh(fx[1], total)
    cond[...] = mmh(scaled.T, scaled)

    def eight(p):
        return rows_at(p * 8, 8)

    cond_out = [copy(cond.at[eight(p)], cond_in.at[me], 5, p, me) for p in peers]
    for c in cond_out:
        c.start()

    def modes(p):
        h, l = yh[own(p), :], yl[own(p), :]
        modes_ref[rows_at(p * 256, 256), :] = mm(cat([h, h, l], 1), ct[...])

    inverse = fx[0]
    turned = inverse.T
    red_ref[...] = mmh(mmh(inverse, sums[1]), turned)
    h, l = split(turned * 256.0)
    ct[...] = cat([h, l, h], 0)
    pairs(modes, 0, 4)
    cond_in[me] = cond[eight(me), :]
    for p in peers:
        copy(cond.at[eight(p)], cond_in.at[p], 5, p, p).wait_recv()
    pieces = [cond_in[i] for i in range(BLK)]
    goals = [jnp.full((8, 128), owned[i], jnp.int32) for i in range(BLK)]
    for g in range(4 * COMP):
        dense[g] = sum(jnp.where(goals[i] == g, pieces[i], 0.0) for i in range(BLK))

    def four(o):
        return pl.ds(o * 4, 4)

    dense_out = [copy(dense.at[four(f)], dense_in.at[mine], 6, f, mine, "comp") for f in friends]
    for c in dense_out:
        c.start()
    pairs(modes, 4, 10)
    acc = dense[four(mine)]
    for f in friends:
        copy(dense.at[four(f)], dense_in.at[f], 6, f, f, "comp").wait_recv()
        acc = acc + dense_in[f]
    slab[...] = acc
    slab_out = [copy(slab, slab_in.at[me], 7, p, me) for p in peers]
    for c in slab_out:
        c.start()
    asm_ref[:, eight(me), :] = acc
    pairs(modes, 10, 16)
    for p in peers:
        copy(slab, slab_in.at[p], 7, p, p).wait_recv()
        asm_ref[:, eight(p), :] = slab_in[p]
    for c in started + w_out + cond_out + dense_out + slab_out:
        c.wait_send()


def result_kernel(*refs):
    modes, red, asm, modes_out, red_out, asm_out, sem = refs
    part = ROWS // PARTS
    moves = [pltpu.make_async_copy(red, red_out, sem.at[PARTS]),
             pltpu.make_async_copy(asm, asm_out, sem.at[PARTS + 1])]
    for i in range(PARTS):
        r = pl.ds(i * part, part)
        moves.append(pltpu.make_async_copy(modes.at[r], modes_out.at[r], sem.at[i]))
    for t in moves:
        t.start()
    for t in moves:
        t.wait()


def local(start_modes, stiff_diag, stiff_off, mass_blocks, coupling, interface_block, global_iface):
    hbm = pl.BlockSpec(memory_space=pltpu.HBM)
    vm = pl.BlockSpec(memory_space=pltpu.VMEM)
    ext = pltpu.VMEM((ROWS + 256, 256), BF)
    blocks = pltpu.VMEM((NB, 128, 128), F32)
    results = pl.pallas_call(
        kernel,
        out_shape=(pltpu.VMEM((ROWS, 256), F32), pltpu.VMEM((256, 256), F32),
                   pltpu.VMEM((4, 128, 128), F32)),
        in_specs=[hbm] * 7,
        out_specs=(vm,) * 3,
        scratch_shapes=[
            pltpu.SMEM((NB,), jnp.int32), pltpu.SMEM((BLK,), jnp.int32),
            pltpu.VMEM((ROWS, 256), F32), blocks, blocks, blocks, blocks,
            ext, ext, ext, ext, ext, ext,
            pltpu.VMEM((NB, 128, 384), BF), pltpu.VMEM((NB, 128, 384), BF),
            pltpu.VMEM((NB + 1, 256, 128), F32),
            pltpu.VMEM((768, 256), BF),
            pltpu.VMEM((4, 128, 256), F32),
            pltpu.VMEM((6, 128, 256), F32),
            pltpu.VMEM((128, 128), F32),
            pltpu.VMEM((2, 256, 256), F32),
            pltpu.VMEM((2, BLK, 16, 256), F32),
            pltpu.VMEM((2, 256, 256), F32),
            pltpu.VMEM((BLK, 256, 128), F32),
            pltpu.VMEM((BLK, 256, 128), F32),
            pltpu.VMEM((2, 256, 256), F32),
            pltpu.VMEM((2, 256, 256), F32),
            pltpu.VMEM((128, 128), F32),
            pltpu.VMEM((BLK, 8, 128), F32),
            pltpu.VMEM((4 * COMP, 8, 128), F32),
            pltpu.VMEM((COMP, 4, 8, 128), F32),
            pltpu.VMEM((4, 8, 128), F32),
            pltpu.VMEM((BLK, 4, 8, 128), F32),
            pltpu.SemaphoreType.DMA((3 * CHUNKS + 4,)),
            pltpu.SemaphoreType.DMA((7,)),
            pltpu.SemaphoreType.DMA((7,)),
            pltpu.SemaphoreType.DMA((8, 16)),
            pltpu.SemaphoreType.DMA((8, 16)),
        ],
        compiler_params=pltpu.CompilerParams(
            collective_id=0, has_side_effects=True, vmem_limit_bytes=54 * MIB),
        name="superelement",
    )(interface_block[0], global_iface[0], start_modes[0], stiff_diag[0], stiff_off[0],
      mass_blocks[0], coupling[0])
    modes, reduced, assembled = pl.pallas_call(
        result_kernel,
        out_shape=(jax.ShapeDtypeStruct((ROWS, 256), F32),
                   jax.ShapeDtypeStruct((256, 256), F32),
                   jax.ShapeDtypeStruct((4, 128, 128), F32)),
        in_specs=[vm] * 3,
        out_specs=(hbm,) * 3,
        scratch_shapes=[pltpu.SemaphoreType.DMA((PARTS + 2,))],
        compiler_params=pltpu.CompilerParams(vmem_limit_bytes=4 * MIB),
        name="result",
    )(*results)
    return modes[None], reduced[None], assembled


def solution(mesh):
    in_specs = (
        P("comp", "blk", None),
        P("comp", "blk", None, None),
        P("comp", "blk", None, None),
        P("comp", "blk", None, None),
        P("comp", "blk", None, None),
        P("comp", "blk"),
        P("comp", None),
    )
    out_specs = (P("comp", "blk", None), P("comp", None, None), P("comp", None, None))
    return jax.shard_map(local, mesh=mesh, in_specs=in_specs, out_specs=out_specs, check_vma=False)
```

```python
import functools

import jax
import jax.numpy as jnp
from jax import lax
from jax.experimental import pallas as pl
from jax.experimental.pallas import tpu as pltpu
from jax.sharding import PartitionSpec as P

BF = jnp.bfloat16
F32 = jnp.float32
STEP = 0.15
MESH = pl.DeviceIdType.MESH
HI = lax.Precision.HIGHEST
MIB = 1 << 20
NB = 32
ROWS = NB * 128
BLK = 16
COMP = 8
CHUNKS = 4
PARTS = 8
EARLY = 6


def split(x):
    hi = x.astype(BF)
    lo = (x - hi.astype(F32)).astype(BF)
    return hi, lo


def mm(a, b):
    return jnp.dot(a, b, preferred_element_type=F32)


def mmh(a, b):
    return jnp.dot(a, b, preferred_element_type=F32, precision=HI)


def cat(parts, axis):
    return jnp.concatenate(parts, axis)


def rows_at(start, size):
    return pl.ds(pl.multiple_of(start, min(size, 128)), size)


def diag_inverse(mats):
    groups = 8
    sub = lax.broadcasted_iota(jnp.int32, (8, 128), 0)
    lane = lax.broadcasted_iota(jnp.int32, (8, 128), 1)
    state = []
    for mat in mats:
        full = cat([mat, jnp.zeros_like(mat)], 1)
        state.append([
            jnp.where(lane == sub + (64 + 8 * g), 1.0, full[8 * g:8 * g + 8]) for g in range(groups)
        ])
    for k in range(groups):
        cols = [[[jnp.broadcast_to(rows[g][:, 8 * k + c:8 * k + c + 1], (8, 128)) for c in range(8)]
                 for g in range(k, groups)] for rows in state]
        for c in range(8):
            for rows, col in zip(state, cols):
                mine = col[0]
                rs = lax.rsqrt(jnp.broadcast_to(mine[c][c:c + 1, :], (8, 128)))
                u = jnp.broadcast_to(rows[k][c:c + 1, :], (8, 128)) * rs
                heads = {n: jnp.broadcast_to(mine[n][c:c + 1, :], (8, 128)) * rs for n in range(c + 1, 8)}
                for g in range(k, groups):
                    mult = col[g - k][c] * rs
                    if g == k:
                        mult = jnp.where(sub > c, mult, 0.0)
                        rows[g] = jnp.where(sub == c, u, rows[g] - mult * u)
                    else:
                        rows[g] = rows[g] - mult * u
                    for n in range(c + 1, 8):
                        col[g - k][n] = col[g - k][n] - mult * heads[n]
    return [cat(rows, 0) for rows in state]


def offsets(me):
    y, z = me // 4, lax.rem(me, 4)
    turns = ((0, 1), (1, 0), (0, 3), (3, 0), (1, 1), (3, 3), (1, 3), (3, 1),
             (0, 2), (2, 0), (1, 2), (2, 1), (3, 2), (2, 3), (2, 2))
    return [lax.rem(y + dy, 4) * 4 + lax.rem(z + dz, 4) for dy, dz in turns]


def kernel(ids_hbm, owned_hbm, x_hbm, d_hbm, e_hbm, m_hbm, c_hbm, modes_ref, red_ref, asm_ref,
           ids, owned, x, d, e, m, cpl, xh, xl, fh, fl, yh, yl, ah, al, cum, ct,
           edge, halo, enext, gram, gram_in, sums, w, w_in, fb,
           cond, cond_in, dense, dense_in, slab, slab_in,
           load_sem, halo_send, halo_recv, send_sem, recv_sem):
    me = lax.axis_index("blk")
    mine = lax.axis_index("comp")
    left, right = lax.rem(me + BLK - 1, BLK), lax.rem(me + 1, BLK)
    peers = offsets(me)
    friends = [lax.rem(mine + k, COMP) for k in range(1, COMP)]
    barrier = pltpu.get_barrier_semaphore()
    for p in peers:
        pl.semaphore_signal(barrier, inc=1, device_id={"blk": p}, device_id_type=MESH)
    for f in friends:
        pl.semaphore_signal(barrier, inc=1, device_id={"comp": f}, device_id_type=MESH)

    step = NB // CHUNKS
    loads = []
    for k in range(CHUNKS):
        b, r = pl.ds(k * step, step), pl.ds(k * step * 128, step * 128)
        trio = [pltpu.make_async_copy(e_hbm.at[b], e.at[b], load_sem.at[3 * k]),
                pltpu.make_async_copy(d_hbm.at[b], d.at[b], load_sem.at[3 * k + 1]),
                pltpu.make_async_copy(x_hbm.at[r], x.at[r], load_sem.at[3 * k + 2])]
        for t in trio:
            t.start()
        loads.append(trio)
    late = [pltpu.make_async_copy(m_hbm, m, load_sem.at[3 * CHUNKS]),
            pltpu.make_async_copy(c_hbm, cpl, load_sem.at[3 * CHUNKS + 1]),
            pltpu.make_async_copy(ids_hbm, ids, load_sem.at[3 * CHUNKS + 2]),
            pltpu.make_async_copy(owned_hbm, owned, load_sem.at[3 * CHUNKS + 3])]

    has_left, has_right = me > 0, me < BLK - 1

    def put_a(b, col, block):
        hi, lo = split(block)
        ah[b, :, col * 128:(col + 1) * 128] = hi
        al[b, :, col * 128:(col + 1) * 128] = lo

    def build(b):
        link = e[b]
        put_a(b, 0, jnp.where(jnp.logical_or(has_left, b > 0), link, 0.0))
        put_a(b, 1, d[b])
        hi, lo = split(x[rows_at(b * 128, 128), :])
        xh[rows_at(b * 128 + 128, 128), :] = hi
        xl[rows_at(b * 128 + 128, 128), :] = lo
        put_a(jnp.where(b > 0, b - 1, NB - 1), 2, link.T)

    def send(src, dst, slot, peer):
        copy = pltpu.make_async_remote_copy(
            src_ref=src, dst_ref=dst, send_sem=halo_send.at[slot], recv_sem=halo_recv.at[slot],
            device_id={"blk": peer}, device_id_type=MESH)
        copy.start()
        return copy

    def copy(src, dst, phase, peer, slot, axis="blk"):
        return pltpu.make_async_remote_copy(
            src_ref=src, dst_ref=dst, send_sem=send_sem.at[phase, peer],
            recv_sem=recv_sem.at[phase, slot], device_id={axis: peer}, device_id_type=MESH)

    def product(vh, vl, p):
        out = []
        for q in range(2):
            s = rows_at(p * 256 + q * 128, 384)
            h, l, a = vh[s, :], vl[s, :], ah[2 * p + q]
            out.append(mm(cat([a, a, al[2 * p + q]], 1), cat([h, l, h], 0)))
        return cat(out, 0)

    def own(p):
        return rows_at(p * 256 + 128, 256)

    def apply_f(p):
        f = x[rows_at(p * 256, 256), :] * (1.0 / 256) - product(xh, xl, p) * (STEP / 256)
        fh[own(p), :], fl[own(p), :] = split(f)
        return f

    def apply_y(p):
        f = fh[own(p), :].astype(F32) + fl[own(p), :].astype(F32)
        y = f - product(fh, fl, p) * STEP
        yh[own(p), :], yl[own(p), :] = split(y)
        return y

    def apply_z(p):
        zh, zl = split(product(yh, yl, p))
        s = rows_at(p * 256, 256)
        th, tl = xh[s, :], xl[s, :]
        gram[1] = gram[1] + mm(cat([th, th, tl], 1), cat([zh, zl, zh], 0))

    def wait_halo(rnd, vh, vl):
        if rnd == 0:
            halos[0].wait()
            put_a(NB - 1, 2, jnp.where(has_right, enext[...], 0.0).T)
        halos[2 * rnd + 1].wait()
        vh[0:128, :], vl[0:128, :] = split(jnp.where(has_left, halo[2 * rnd], 0.0))
        halos[2 * rnd + 2].wait()
        vh[ROWS + 128:ROWS + 256, :], vl[ROWS + 128:ROWS + 256, :] = split(
            jnp.where(has_right, halo[2 * rnd + 1], 0.0))

    def pairs(fn, start, stop):
        def body(i, _):
            fn(start + 2 * i)
            fn(start + 2 * i + 1)
            return 0

        lax.fori_loop(0, (stop - start) // 2, body, 0)

    last_pair = NB // 2 - 1
    for k in range(CHUNKS):
        for t in loads[k]:
            t.wait()
        if k == 2:
            for t in late:
                t.start()
            pl.semaphore_wait(barrier, len(peers) + len(friends))
            halos = [
                send(e_hbm.at[0], enext, 6, left),
                send(x_hbm.at[pl.ds(ROWS - 128, 128)], halo.at[0], 0, right),
                send(x_hbm.at[pl.ds(0, 128)], halo.at[1], 1, left),
            ]
        first = k * step // 2
        if k == 0:
            for p in range(3):
                build(2 * p)
                build(2 * p + 1)
            apply_f(1)
            build(6)
            build(7)
        else:
            def both(i, _, first=first):
                for u in range(2):
                    p = first + 2 * i + u
                    apply_f(p - 2)
                    build(2 * p)
                    build(2 * p + 1)
                return 0

            lax.fori_loop(0, step // 4, both, 0)
    apply_f(last_pair - 1)

    for rnd, (fn, vh, vl) in enumerate(((apply_f, xh, xl), (apply_y, fh, fl))):
        if rnd:
            pairs(fn, 1, last_pair)
        wait_halo(rnd, vh, vl)
        edge[2 * rnd] = fn(last_pair)[128:, :]
        halos.append(send(edge.at[2 * rnd], halo.at[2 * rnd + 2], 2 * rnd + 2, right))
        edge[2 * rnd + 1] = fn(0)[:128, :]
        halos.append(send(edge.at[2 * rnd + 1], halo.at[2 * rnd + 3], 2 * rnd + 3, left))

    for t in late:
        t.wait()
    gram[...] = jnp.zeros_like(gram)
    cum[0] = jnp.zeros((256, 128), F32)

    def before(b):
        slot = 0
        for q in range(NB):
            slot = jnp.where(jnp.logical_and(ids[q] == ids[b], q < b), q + 1, slot)
        return slot

    def final(j):
        slot = 0
        for q in range(NB):
            slot = jnp.where(ids[q] == j, q + 1, slot)
        return slot

    def mass(p):
        h, l = yh[own(p), :], yl[own(p), :]
        parts = []
        for q in range(2):
            mh, ml = split(m[2 * p + q])
            s = slice(q * 128, (q + 1) * 128)
            both = mm(cat([cat([mh, mh], 1), cat([ml, ml], 1)], 0), cat([h[s], l[s]], 0))
            parts.append(both[:128] + both[128:])
        mh, ml = split(cat(parts, 0))
        th, tl = h.T, l.T
        xh[rows_at(p * 256, 256), :] = th
        xl[rows_at(p * 256, 256), :] = tl
        gram[0] = gram[0] + mm(cat([th, th, tl], 1), cat([mh, ml, mh], 0))
        for q in range(2):
            b = 2 * p + q
            ch, cl = split(cpl[b])
            cc = cat([ch, cl], 1)
            s = slice(q * 128, (q + 1) * 128)
            both = mm(cat([th[:, s], tl[:, s]], 1), cat([cc, cc], 0))
            cum[b + 1] = both[:, :128] + both[:, 128:] + cum[before(b)]

    pairs(mass, 0, NB // 2)

    def part(p):
        return rows_at(p * 16, 16)

    def reduce_out(t):
        out = [copy(gram.at[t, part(p)], gram_in.at[t, me], t, p, me) for p in peers]
        for c in out:
            c.start()
        return out

    def reduce_in(t):
        acc = gram[t, part(me), :]
        for p in peers:
            copy(gram.at[t, part(p)], gram_in.at[t, p], t, p, p).wait_recv()
            acc = acc + gram_in[t, p]
        sums[t, part(me), :] = acc
        piece = sums.at[t, part(me)]
        out = [copy(piece, piece, 2 + t, p, me) for p in peers]
        for c in out:
            c.start()
        return out

    def gathered(t):
        for p in peers:
            copy(sums.at[t, part(me)], sums.at[t, part(p)], 2 + t, p, p).wait_recv()

    started = reduce_out(0)

    def projection(j, _):
        w[j] = cum[final(j)]
        return 0

    lax.fori_loop(0, BLK, projection, 0)
    w_out = [copy(w.at[p], w_in.at[me], 4, p, me) for p in peers]
    for c in w_out[:EARLY]:
        c.start()

    pairs(apply_z, 1, 11)
    started += reduce_in(0)
    pairs(apply_z, 11, last_pair)
    wait_halo(2, yh, yl)
    apply_z(0)
    apply_z(last_pair)
    started += reduce_out(1)
    started += reduce_in(1)
    for c in w_out[EARLY:]:
        c.start()
    gathered(0)
    gathered(1)

    size = 256
    column = lax.broadcasted_iota(jnp.int32, (size, size), 1)
    row = lax.broadcasted_iota(jnp.int32, (size, size), 0)
    for t in range(2):
        g = sums[t]
        fb[t] = (g + g.T) * 0.5
    for k in range(4):
        lo, hi = 64 * k, 64 * (k + 1)
        inv = diag_inverse([fb[t, lo:hi, lo:hi] for t in range(2)])
        inside = jnp.logical_and(column >= lo, column < hi)
        for t in range(2):
            unit = jnp.where(column[:64] == row[:64] + lo, 1.0, 0.0)
            u = mmh(inv[t][:, 64:], jnp.where(inside[:64], unit, fb[t, lo:hi, :]))
            fb[t, lo:hi, :] = u
            if k < 3:
                low = u.T[hi:, :]
                fb[t, hi:, :] = jnp.where(inside[hi:], 0.0, fb[t, hi:, :]) - mmh(low, u)
    lower = column // 64 <= row // 64

    def inverse_of(t):
        return jnp.where(lower, fb[t], 0.0)

    total = w[me]
    for p in peers:
        copy(w.at[p], w_in.at[p], 4, p, p).wait_recv()
        total = total + w_in[p]
    scaled = mmh(inverse_of(1), total)
    cond[...] = mmh(scaled.T, scaled)

    def eight(p):
        return rows_at(p * 8, 8)

    cond_out = [copy(cond.at[eight(p)], cond_in.at[me], 5, p, me) for p in peers]
    for c in cond_out:
        c.start()

    def modes(p):
        h, l = yh[own(p), :], yl[own(p), :]
        modes_ref[rows_at(p * 256, 256), :] = mm(cat([h, h, l], 1), ct[...])

    inverse = inverse_of(0)
    turned = inverse.T
    h, l = split(turned * 256.0)
    ct[...] = cat([h, l, h], 0)
    pairs(modes, 0, 4)
    cond_in[me] = cond[eight(me), :]
    for p in peers:
        copy(cond.at[eight(p)], cond_in.at[p], 5, p, p).wait_recv()
    pieces = [cond_in[i] for i in range(BLK)]
    goals = [jnp.full((8, 128), owned[i], jnp.int32) for i in range(BLK)]
    for g in range(4 * COMP):
        dense[g] = sum(jnp.where(goals[i] == g, pieces[i], 0.0) for i in range(BLK))

    def four(o):
        return pl.ds(o * 4, 4)

    dense_out = [copy(dense.at[four(f)], dense_in.at[mine], 6, f, mine, "comp") for f in friends]
    for c in dense_out:
        c.start()
    pairs(modes, 4, 10)
    acc = dense[four(mine)]
    for f in friends:
        copy(dense.at[four(f)], dense_in.at[f], 6, f, f, "comp").wait_recv()
        acc = acc + dense_in[f]
    slab[...] = acc
    slab_out = [copy(slab, slab_in.at[me], 7, p, me) for p in peers]
    for c in slab_out:
        c.start()
    asm_ref[:, eight(me), :] = acc
    red_ref[...] = mmh(mmh(inverse, sums[1]), turned)
    pairs(modes, 10, 16)
    for c in started + w_out + cond_out + dense_out:
        c.wait_send()
    for p in peers:
        copy(slab, slab_in.at[p], 7, p, p).wait_recv()
        asm_ref[:, eight(p), :] = slab_in[p]
    for c in slab_out:
        c.wait_send()


def result_kernel(*refs):
    modes, red, asm, modes_out, red_out, asm_out, sem = refs
    part = ROWS // PARTS
    moves = [pltpu.make_async_copy(red, red_out, sem.at[PARTS]),
             pltpu.make_async_copy(asm, asm_out, sem.at[PARTS + 1])]
    for i in range(PARTS):
        r = pl.ds(i * part, part)
        moves.append(pltpu.make_async_copy(modes.at[r], modes_out.at[r], sem.at[i]))
    for t in moves:
        t.start()
    for t in moves:
        t.wait()


def local(start_modes, stiff_diag, stiff_off, mass_blocks, coupling, interface_block, global_iface):
    hbm = pl.BlockSpec(memory_space=pltpu.HBM)
    vm = pl.BlockSpec(memory_space=pltpu.VMEM)
    ext = pltpu.VMEM((ROWS + 256, 256), BF)
    blocks = pltpu.VMEM((NB, 128, 128), F32)
    results = pl.pallas_call(
        kernel,
        out_shape=(pltpu.VMEM((ROWS, 256), F32), pltpu.VMEM((256, 256), F32),
                   pltpu.VMEM((4, 128, 128), F32)),
        in_specs=[hbm] * 7,
        out_specs=(vm,) * 3,
        scratch_shapes=[
            pltpu.SMEM((NB,), jnp.int32), pltpu.SMEM((BLK,), jnp.int32),
            pltpu.VMEM((ROWS, 256), F32), blocks, blocks, blocks, blocks,
            ext, ext, ext, ext, ext, ext,
            pltpu.VMEM((NB, 128, 384), BF), pltpu.VMEM((NB, 128, 384), BF),
            pltpu.VMEM((NB + 1, 256, 128), F32),
            pltpu.VMEM((768, 256), BF),
            pltpu.VMEM((4, 128, 256), F32),
            pltpu.VMEM((6, 128, 256), F32),
            pltpu.VMEM((128, 128), F32),
            pltpu.VMEM((2, 256, 256), F32),
            pltpu.VMEM((2, BLK, 16, 256), F32),
            pltpu.VMEM((2, 256, 256), F32),
            pltpu.VMEM((BLK, 256, 128), F32),
            pltpu.VMEM((BLK, 256, 128), F32),
            pltpu.VMEM((2, 256, 256), F32),
            pltpu.VMEM((128, 128), F32),
            pltpu.VMEM((BLK, 8, 128), F32),
            pltpu.VMEM((4 * COMP, 8, 128), F32),
            pltpu.VMEM((COMP, 4, 8, 128), F32),
            pltpu.VMEM((4, 8, 128), F32),
            pltpu.VMEM((BLK, 4, 8, 128), F32),
            pltpu.SemaphoreType.DMA((3 * CHUNKS + 4,)),
            pltpu.SemaphoreType.DMA((7,)),
            pltpu.SemaphoreType.DMA((7,)),
            pltpu.SemaphoreType.DMA((8, 16)),
            pltpu.SemaphoreType.DMA((8, 16)),
        ],
        compiler_params=pltpu.CompilerParams(
            collective_id=0, has_side_effects=True, vmem_limit_bytes=54 * MIB),
        name="superelement",
    )(interface_block[0], global_iface[0], start_modes[0], stiff_diag[0], stiff_off[0],
      mass_blocks[0], coupling[0])
    modes, reduced, assembled = pl.pallas_call(
        result_kernel,
        out_shape=(jax.ShapeDtypeStruct((ROWS, 256), F32),
                   jax.ShapeDtypeStruct((256, 256), F32),
                   jax.ShapeDtypeStruct((4, 128, 128), F32)),
        in_specs=[vm] * 3,
        out_specs=(hbm,) * 3,
        scratch_shapes=[pltpu.SemaphoreType.DMA((PARTS + 2,))],
        compiler_params=pltpu.CompilerParams(vmem_limit_bytes=4 * MIB),
        name="result",
    )(*results)
    return modes[None], reduced[None], assembled


def solution(mesh):
    in_specs = (
        P("comp", "blk", None),
        P("comp", "blk", None, None),
        P("comp", "blk", None, None),
        P("comp", "blk", None, None),
        P("comp", "blk", None, None),
        P("comp", "blk"),
        P("comp", None),
    )
    out_specs = (P("comp", "blk", None), P("comp", None, None), P("comp", None, None))
    return jax.shard_map(local, mesh=mesh, in_specs=in_specs, out_specs=out_specs, check_vma=False)
```
